32 devices in a mesh: panel: 4 (over y, x), inc: 8 (over z, core).
Axes of the slice: x: 2, y: 2, z: 4, core: 2. Of those that a mesh axis runs over, the one named last changes fastest.
Arguments:
- surface_field: bfloat16 [2, 128, 2048], P(None, 'inc', 'panel'), may hold values from -6 to 6
- near_block: bfloat16 [16, 128, 8, 2, 128], P('panel', 'inc'), may hold values from -0.125 to 0.125
- near_index: int32 [16, 8], P('panel'), may hold values from 0 to 15, as said below
- source_basis: bfloat16 [16, 2, 16, 128], P('panel'), may hold values from -0.375 to 0.375
- coupling: bfloat16 [16, 2, 16, 256], P('panel'), may hold values from -0.375 to 0.375
- target_basis: bfloat16 [16, 2, 16, 128], P('panel'), may hold values from -1 to 1
- far_rank: int32 [16, 16], P('panel'), may hold values from 1 to 16, as said below
Outputs:
- applied_field: bfloat16 [2, 128, 2048], P(None, 'inc', 'panel')
The draws below stay inside these ranges and needn't reach their ends.
Inputs may be any that keep to these rules, and one draw needn't show every extreme that they name: `near_index`: each row names 8 distinct blocks within 4 blocks of its own block i around the closed order of blocks (index modulo 16); slot 0 names i, slot 1 names i - 4 and slot 2 names i + 4. `far_rank`: entries of pairs named in near_index are not used; every block i has rank 16 toward block i + 8.
All inputs are finite; a program needn't handle non-finite values.
Results may differ from the reference program's by a relative error of at most 0.0042.
Values may be sent and summed in bfloat16 or wider, within the bound.
No kernel may reach another device: no remote copies, remote signals or barrier semaphores. Data moves between devices by JAX's collectives and lax.ppermute only.
A program may use at most 64 MiB of HBM per device.

```python
import jax
import jax.numpy as jnp
from jax import lax

BLK = 128
KN = 8
RMAX = 16
BPD = 4
NB = 16
PANELS = 2048
INC = 128


def draw_near_index(key, part):
    reach = BPD
    ahead = jnp.arange(1, reach, dtype=jnp.int32)
    candidates = jnp.concatenate([ahead, -ahead])
    keys = jax.random.split(key, NB)
    shuffled = jax.vmap(lambda single: jax.random.permutation(single, candidates))(keys)
    chosen = shuffled[:, :KN - 3]
    fixed = jnp.broadcast_to(jnp.array([0, -reach, reach], dtype=jnp.int32), (NB, 3))
    offsets = jnp.concatenate([fixed, chosen], axis=1)
    return (jnp.arange(NB, dtype=jnp.int32)[:, None] + offsets) % NB


def draw_far_rank(key, part):
    ranks = jax.random.randint(key, (NB, NB), 1, RMAX + 1, dtype=jnp.int32)
    rows = jnp.arange(NB, dtype=jnp.int32)[:, None]
    cols = jnp.arange(NB, dtype=jnp.int32)[None, :]
    partner = (rows + NB // 2) % NB
    return jnp.where(cols == partner, RMAX, ranks).astype(jnp.int32)


def block_scale(own_key, shape, cuts, smallest, high):
    def one(axis_at, shards_of):
        heights = jax.random.uniform(jax.random.fold_in(jax.random.fold_in(own_key, 6), axis_at), (shards_of,), jnp.float32, smallest / len(cuts), high / len(cuts))
        return jnp.repeat(jnp.exp(heights), shape[axis_at] // shards_of).reshape((-1,) + (1,) * (len(shape) - axis_at - 1))

    gain = one(*cuts[0])
    for cut in cuts[1:]:
        gain = gain * one(*cut)
    return gain


def scatter_about(stream_key, dims, spread, limit, shards=(), kind=jnp.bfloat16):
    values = jax.random.normal(stream_key, dims, jnp.float32) * spread
    if len(shards) > 0:
        values = block_scale(stream_key, dims, shards, -0.22, 0.18) * values
    return jnp.clip(values, min=-limit, max=limit).astype(kind)


def setup_inputs(seed: int = 0) -> dict:
    splits = jax.random.split(jax.random.key(seed), 8)
    return {
        "surface_field": scatter_about(splits[0], (2, INC, PANELS), 1.0, 6.0, ((1, 8), (2, 4))),
        "near_block": scatter_about(splits[1], (NB, BLK, KN, 2, BLK), (2 * KN * BLK) ** -0.5, 0.125, ((0, 4), (1, 8))),
        "near_index": draw_near_index(jax.random.fold_in(splits[7], 71), 0),
        "source_basis": scatter_about(splits[3], (NB, 2, RMAX, BLK), (2 * BLK) ** -0.5, 0.375, ((0, 4),)),
        "coupling": scatter_about(splits[4], (NB, 2, RMAX, NB * RMAX), (NB * RMAX) ** -0.5, 0.375, ((0, 4),)),
        "target_basis": scatter_about(splits[5], (NB, 2, RMAX, BLK), (2 * RMAX) ** -0.5, 1.0, ((0, 4),)),
        "far_rank": draw_far_rank(jax.random.fold_in(splits[7], 71), 0),
    }


def reference(surface_field, near_block, near_index, source_basis, coupling, target_basis, far_rank):
    field_float = surface_field.astype(jnp.float32)
    field_blocks = field_float.reshape(2, INC, NB, BLK)
    vreal = source_basis[:, 0].astype(jnp.float32)
    vimag = source_basis[:, 1].astype(jnp.float32)
    part_a = jnp.einsum('jas,pmjs->pjam', vreal, field_blocks)
    part_b = jnp.einsum('jas,pmjs->pjam', vimag, field_blocks)
    compressed = jnp.stack([part_a[0] - part_b[1], part_a[1] + part_b[0]]).astype(jnp.bfloat16)
    compressed = compressed.reshape(2, NB * RMAX, INC).astype(jnp.float32)

    columns = jnp.arange(NB * RMAX, dtype=jnp.int32)
    within = columns % RMAX
    block_ids = jnp.arange(NB, dtype=jnp.int32)
    is_near = jnp.any(near_index[:, :, None] == block_ids[None, None, :], axis=1)
    rank_cols = jnp.repeat(far_rank, RMAX, axis=1)
    near_cols = jnp.repeat(is_near, RMAX, axis=1)
    rows_a = jnp.arange(RMAX, dtype=jnp.int32)
    keep = (rows_a[None, :, None] < rank_cols[:, None, :]) & (within[None, None, :] < rank_cols[:, None, :]) & jnp.logical_not(near_cols[:, None, :])
    masked = (coupling.astype(jnp.float32) * keep[:, None].astype(jnp.float32))
    part_a = jnp.einsum('iac,pcn->pian', masked[:, 0], compressed)
    part_b = jnp.einsum('iac,pcn->pian', masked[:, 1], compressed)
    mixed = jnp.stack([part_a[0] - part_b[1], part_a[1] + part_b[0]]).astype(jnp.bfloat16).astype(jnp.float32)
    ureal = target_basis[:, 0].astype(jnp.float32)
    uimag = target_basis[:, 1].astype(jnp.float32)
    part_a = jnp.einsum('iat,pian->pnit', ureal, mixed)
    part_b = jnp.einsum('iat,pian->pnit', uimag, mixed)
    far = jnp.stack([part_a[0] - part_b[1], part_a[1] + part_b[0]])

    def one_block(operands):
        coefs, picks = operands
        source = jnp.take(field_blocks, picks.astype(jnp.int32), axis=2)
        first_a = jnp.einsum('rks,pmks->pmr', coefs[:, :, 0].astype(jnp.float32), source)
        first_b = jnp.einsum('rks,pmks->pmr', coefs[:, :, 1].astype(jnp.float32), source)
        return jnp.stack([first_a[0] - first_b[1], first_a[1] + first_b[0]])

    near = lax.map(one_block, (near_block, near_index))
    near = jnp.transpose(near, (1, 2, 0, 3))
    result = field_blocks * 0.5 + near + far
    return result.reshape(2, INC, PANELS).astype(jnp.bfloat16)
```

```python
import functools

import jax
import jax.numpy as jnp
from jax import lax
from jax.experimental import pallas as pl
from jax.experimental.pallas import tpu as pltpu
from jax.sharding import PartitionSpec as P

F32 = jnp.float32
BF16 = jnp.bfloat16
LANES = 128
VMEM = pl.BlockSpec(memory_space=pltpu.VMEM)
SMEM = pl.BlockSpec(memory_space=pltpu.SMEM)
PARAMS = pltpu.CompilerParams(vmem_limit_bytes=8 * 1024 * 1024)


def nt_dot(left, right):
    return lax.dot_general(left, right, (((1,), (1,)), ((), ())), preferred_element_type=F32)


def tn_dot(left, right):
    return lax.dot_general(left, right, (((0,), (0,)), ((), ())), preferred_element_type=F32)


def times_i(pair_rows, width):
    return jnp.concatenate([-pair_rows[width:], pair_rows[:width]], axis=0)


def times_i_lanes(pair_lanes, width):
    return jnp.concatenate([-pair_lanes[:, width:], pair_lanes[:, :width]], axis=1)


def pack_kernel(own_ref, other_ref, basis_ref, payload_ref, packed_ref):
    _, inc, panels = own_ref.shape
    blocks, _, rank, block = basis_ref.shape
    for part in range(2):
        payload_ref[part * inc : (part + 1) * inc, :panels] = own_ref[part]
        payload_ref[(2 + part) * inc : (3 + part) * inc, :panels] = other_ref[part]
    if payload_ref.shape[0] > 4 * inc:
        payload_ref[4 * inc :, :panels] = jnp.zeros((payload_ref.shape[0] - 4 * inc, panels), BF16)
    pieces = []
    for j in range(blocks):
        basis = jnp.concatenate([basis_ref[j, 0], basis_ref[j, 1]], axis=0)
        field = jnp.concatenate(
            [own_ref[part][:, j * block : (j + 1) * block] for part in range(2)], axis=0
        )
        both = nt_dot(basis, field)
        pieces.append(both[:rank] + times_i_lanes(both[rank:], inc))
    compressed = jnp.concatenate(pieces, axis=0)
    pad = packed_ref.shape[1] - 2 * inc
    compressed = jnp.concatenate([compressed, jnp.zeros((blocks * rank, pad), F32)], axis=1)
    compressed = compressed.astype(BF16)
    packed_ref[...] = compressed
    payload_ref[: blocks * rank, panels:] = compressed
    if payload_ref.shape[0] > blocks * rank:
        payload_ref[blocks * rank :, panels:] = jnp.zeros(
            (payload_ref.shape[0] - blocks * rank, packed_ref.shape[1]), BF16
        )


def near_kernel(pieces, inc, block, slots, *refs):
    picks_ref = refs[0]
    window_refs = refs[1:4]
    coefs_refs = refs[4 : 4 + pieces]
    keep_ref, send_ref, wide_ref = refs[4 + pieces :]
    blocks = coefs_refs[0].shape[0]
    rows = 4 * inc
    for w in range(3):
        piece = window_refs[w][:rows, : blocks * block]
        turned = jnp.concatenate(
            [times_i(piece[: 2 * inc], inc), times_i(piece[2 * inc :], inc)], axis=0
        )
        for b in range(blocks):
            at = (w * blocks + b) * 2 * block
            wide_ref[:, at : at + block] = piece[:, b * block : (b + 1) * block]
            wide_ref[:, at + block : at + 2 * block] = turned[:, b * block : (b + 1) * block]
    for i in range(blocks):
        total = None
        for k in range(slots):
            start = pl.multiple_of(picks_ref[i, k] * (2 * block), 2 * block)
            field = wide_ref[:, pl.ds(start, 2 * block)]
            span = slice(k * 2 * block, (k + 1) * 2 * block)
            coefs = [ref[i, :, span] for ref in coefs_refs]
            coefs = coefs[0] if pieces == 1 else jnp.concatenate(coefs, axis=0)
            term = nt_dot(field, coefs)
            total = term if total is None else total + term
        width = total.shape[1]
        keep_ref[:, i * width : (i + 1) * width] = total[: 2 * inc]
        send_ref[:, i * width : (i + 1) * width] = total[2 * inc :].astype(BF16)


def far_kernel(count, inc, index_ref, near_ref, rank_ref, coupling_ref, target_ref, *refs):
    piece_refs = refs[:count]
    far_ref, gathered_ref = refs[count:]
    blocks, _, rank, columns = coupling_ref.shape
    block = target_ref.shape[3]
    size = blocks * rank
    me = index_ref[0]
    for k in range(count):
        at = lax.rem(me + k, count) * size
        at = pl.multiple_of(at, size)
        ref = piece_refs[k]
        lane = ref.shape[1] - gathered_ref.shape[1]
        gathered_ref[pl.ds(at, size), :] = ref[:size, lane:]
    block_id = lax.broadcasted_iota(jnp.int32, (rank, columns), 1) // rank
    within = lax.broadcasted_iota(jnp.int32, (rank, columns), 1) % rank
    row = lax.broadcasted_iota(jnp.int32, (rank, columns), 0)
    largest = jnp.maximum(within, row)
    masked = [[], []]
    for i in range(blocks):
        ranks = jnp.zeros((rank, columns), jnp.int32)
        for j in range(columns // rank):
            ranks = jnp.where(block_id == j, rank_ref[i, j], ranks)
        keep = largest < ranks
        for k in range(near_ref.shape[1]):
            keep = keep & (block_id != near_ref[i, k])
        for part in range(2):
            value = coupling_ref[i, part].astype(F32)
            masked[part].append(jnp.where(keep, value, 0.0).astype(BF16))
    masked = jnp.concatenate(masked[0] + masked[1], axis=0)
    both = jnp.dot(masked, gathered_ref[...], preferred_element_type=F32)[:, : 2 * inc]
    mixed = (both[:size] + times_i_lanes(both[size:], inc)).astype(BF16).astype(F32)
    mixed = jnp.concatenate([mixed, times_i_lanes(mixed, inc)], axis=0).astype(BF16)
    row_block = lax.broadcasted_iota(jnp.int32, (size, block), 0) // rank
    basis = [
        jnp.concatenate([target_ref[i, part] for i in range(blocks)], axis=0).astype(F32)
        for part in range(2)
    ]
    spread = [
        jnp.concatenate(
            [jnp.where(row_block == i, basis[part], 0.0) for part in range(2)], axis=0
        ).astype(BF16)
        for i in range(blocks)
    ]
    for i in range(blocks):
        far_ref[:, i * block : (i + 1) * block] = tn_dot(mixed, spread[i])


def final_kernel(count, rows, index_ref, field_ref, keep_ref, got_ref, far_ref, out_ref):
    _, inc, panels = field_ref.shape
    block = count * rows
    half = block // 2
    lane = lax.broadcasted_iota(jnp.int32, (2 * inc, block), 1)
    me = index_ref[1]
    for i in range(panels // block):
        span = slice(i * block, (i + 1) * block)
        part = slice(i * half, (i + 1) * half)
        near = jnp.concatenate([keep_ref[:, part], got_ref[:, part].astype(F32)], axis=1)
        bit = 1
        while bit < count:
            shift = bit * rows
            upper = (lane // shift) % 2 == 1
            swapped = jnp.where(
                upper, pltpu.roll(near, shift, 1), pltpu.roll(near, block - shift, 1)
            )
            near = jnp.where((me // bit) % 2 == 1, swapped, near)
            bit *= 2
        field = jnp.concatenate([field_ref[0][:, span], field_ref[1][:, span]], axis=0)
        result = (field.astype(F32) * 0.5 + near + far_ref[:, span]).astype(BF16)
        out_ref[0, :, span] = result[:inc]
        out_ref[1, :, span] = result[inc:]


def local(surface_field, near_block, near_index, source_basis, coupling, target_basis, far_rank):
    blocks, rows, slots, _, block = near_block.shape
    _, inc, panels = surface_field.shape
    rank = source_basis.shape[2]
    panel_count = lax.axis_size("panel")
    inc_count = lax.axis_size("inc")
    half = inc_count // 2
    panel_at = lax.axis_index("panel")
    inc_at = lax.axis_index("inc")

    def across(x, bit):
        return lax.ppermute(x, "inc", [(i, i ^ bit) for i in range(inc_count)])

    def onward(x, step):
        return lax.ppermute(
            x, "panel", [(i, (i - step) % panel_count) for i in range(panel_count)]
        )

    local_ids = jnp.arange(blocks, dtype=jnp.int32)[:, None]
    offsets = (near_index - (panel_at * blocks + local_ids) + blocks) % (panel_count * blocks)
    picks = jnp.minimum(offsets + local_ids, 3 * blocks - 1)
    index = jnp.stack([panel_at, inc_at]).astype(jnp.int32)

    other = across(surface_field, half)
    coefs = {0: near_block.reshape(blocks, rows, slots * 2 * block)}
    bit = half // 2
    while bit:
        for at in sorted(coefs):
            coefs[at | bit] = across(coefs[at], bit)
        bit //= 2
    coefs = [coefs[at] for at in range(half)]
    if rows % 16:
        coefs = [jnp.concatenate(coefs, axis=1)]

    height = max(4 * inc, blocks * rank)
    pad = -(-2 * inc // LANES) * LANES
    payload, packed = pl.pallas_call(
        pack_kernel,
        out_shape=(
            jax.ShapeDtypeStruct((height, panels + pad), BF16),
            jax.ShapeDtypeStruct((blocks * rank, pad), BF16),
        ),
        in_specs=[VMEM] * 3,
        out_specs=(VMEM, VMEM),
        compiler_params=PARAMS,
        name="pack",
    )(surface_field, other, source_basis)
    above = onward(payload, 1)
    below = onward(payload, panel_count - 1)
    rest = [onward(packed, k) for k in range(2, panel_count - 1)]

    width = blocks * half * rows
    keep, send = pl.pallas_call(
        functools.partial(near_kernel, len(coefs), inc, block, slots),
        out_shape=(
            jax.ShapeDtypeStruct((2 * inc, width), F32),
            jax.ShapeDtypeStruct((2 * inc, width), BF16),
        ),
        in_specs=[SMEM] + [VMEM] * (3 + len(coefs)),
        out_specs=(VMEM, VMEM),
        scratch_shapes=[pltpu.VMEM((4 * inc, 3 * blocks * 2 * block), BF16)],
        compiler_params=PARAMS,
        name="near",
    )(picks, below, payload, above, *coefs)
    got = across(send, half)

    far = pl.pallas_call(
        functools.partial(far_kernel, panel_count, inc),
        out_shape=jax.ShapeDtypeStruct((2 * inc, panels), F32),
        in_specs=[SMEM] * 3 + [VMEM] * (2 + panel_count),
        out_specs=VMEM,
        scratch_shapes=[pltpu.VMEM((panel_count * blocks * rank, pad), BF16)],
        compiler_params=PARAMS,
        name="far",
    )(index, near_index, far_rank, coupling, target_basis, packed, above, *rest, below)

    return pl.pallas_call(
        functools.partial(final_kernel, inc_count, rows),
        out_shape=jax.ShapeDtypeStruct((2, inc, panels), BF16),
        in_specs=[SMEM] + [VMEM] * 4,
        out_specs=VMEM,
        compiler_params=PARAMS,
        name="final",
    )(index, surface_field, keep, got, far)


def solution(mesh):
    return jax.shard_map(
        local,
        mesh=mesh,
        in_specs=(
            P(None, "inc", "panel"),
            P("panel", "inc", None, None, None),
            P("panel", None),
            P("panel", None, None, None),
            P("panel", None, None, None),
            P("panel", None, None, None),
            P("panel", None),
        ),
        out_specs=P(None, "inc", "panel"),
        check_vma=False,
    )
```

```python
import functools

import jax
import jax.numpy as jnp
from jax import lax
from jax.experimental import pallas as pl
from jax.experimental.pallas import tpu as pltpu
from jax.sharding import PartitionSpec as P

F32 = jnp.float32
BF16 = jnp.bfloat16
VMEM = pl.BlockSpec(memory_space=pltpu.VMEM)
SMEM = pl.BlockSpec(memory_space=pltpu.SMEM)
ANY = pl.BlockSpec(memory_space=pl.ANY)


TURN = 3.0
TURN2 = 3.0


def params():
    return pltpu.CompilerParams(vmem_limit_bytes=8 * 1024 * 1024)


def cost(us):
    return pl.CostEstimate(flops=int(us * 1e9), bytes_accessed=0, transcendentals=0)


def in_hbm(x):
    return pltpu.with_memory_space_constraint(x, pltpu.HBM)


def nt_dot(left, right):
    return lax.dot_general(left, right, (((1,), (1,)), ((), ())), preferred_element_type=F32)


def tn_dot(left, right):
    return lax.dot_general(left, right, (((0,), (0,)), ((), ())), preferred_element_type=F32)


def times_i(pair_rows, width):
    return jnp.concatenate([-pair_rows[width:], pair_rows[:width]], axis=0)


def times_i_lanes(pair_lanes, width):
    return jnp.concatenate([-pair_lanes[:, width:], pair_lanes[:, :width]], axis=1)


def compress_kernel(field_hbm, basis_hbm, packed_ref, field_ref, basis_ref, sems):
    copies = [
        pltpu.make_async_copy(field_hbm, field_ref, sems.at[0]),
        pltpu.make_async_copy(basis_hbm, basis_ref, sems.at[1]),
    ]
    for copy in copies:
        copy.start()
    for copy in copies:
        copy.wait()
    _, inc, _ = field_ref.shape
    blocks, _, rank, block = basis_ref.shape
    pieces = []
    for j in range(blocks):
        basis = jnp.concatenate([basis_ref[j, 0], basis_ref[j, 1]], axis=0)
        field = jnp.concatenate(
            [field_ref[part][:, j * block : (j + 1) * block] for part in range(2)], axis=0
        )
        both = nt_dot(basis, field)
        pieces.append(both[:rank] + times_i_lanes(both[rank:], inc))
    packed_ref[...] = jnp.concatenate(pieces, axis=1).astype(BF16)


def pack_kernel(own_ref, other_ref, packed_ref, payload_ref, again_ref):
    _, inc, panels = own_ref.shape
    block = payload_ref.shape[1]
    for b in range(panels // block):
        for side, ref in enumerate((own_ref, other_ref)):
            for part in range(2):
                at = ((b * 2 + side) * 2 + part) * inc
                payload_ref[at : at + inc, :] = ref[part][:, b * block : (b + 1) * block]
    payload_ref[4 * inc * (panels // block) :, :] = packed_ref[...]
    again_ref[...] = packed_ref[...]


def fill_wide(wide_ref, window_refs, inc, blocks, block):
    for w, refs in enumerate(window_refs):
        for b in range(blocks):
            span = slice(b * 4 * inc, (b + 1) * 4 * inc)
            piece = refs[0][span, :]
            if len(refs) == 2:
                odd = lax.rem(lax.axis_index("panel"), 2) == 1
                piece = jnp.where(odd, refs[1][span, :], piece)
            turned = jnp.concatenate(
                [times_i(piece[: 2 * inc], inc), times_i(piece[2 * inc :], inc)], axis=0
            )
            at = (w * blocks + b) * 2 * block
            wide_ref[:, at : at + block] = piece
            wide_ref[:, at + block : at + 2 * block] = turned


def pick_matrix(near_ref, i, rows, slots, blocks, panel_count):
    total = blocks * panel_count
    shape = ((2 * blocks + 1) * 2 * rows, rows * slots * 2)
    out = lax.broadcasted_iota(jnp.int32, shape, 0)
    col = lax.broadcasted_iota(jnp.int32, (1, shape[1]), 1)
    slot = (col // 2) % slots
    distance = jnp.zeros((1, shape[1]), jnp.int32)
    for k in range(slots):
        distance = jnp.where(slot == k, near_ref[i : i + 1, k : k + 1], distance)
    distance = distance - (lax.axis_index("panel") * blocks + i) + blocks
    distance = jnp.where(distance < 0, distance + total, distance)
    distance = jnp.where(distance >= total, distance - total, distance)
    source = (distance * 2 + col % 2) * rows + col // (2 * slots)
    return jnp.where(out == source, 1.0, 0.0).astype(BF16)


def turn(pick, piece_ref, i):
    lines = pick.shape[1]
    piece = piece_ref[i * lines : (i + 1) * lines, :]
    return jnp.dot(pick, piece, preferred_element_type=F32).astype(BF16)


def turn_first_kernel(sizes, near_ref, *refs):
    rows, slots, block, blocks, panel_count, swaps = sizes
    own_ref, mate_ref = refs[:2]
    pick_ref, own_out, mate_out = refs[-3:]
    for i in range(blocks):
        pick = pick_matrix(near_ref, i, rows, slots, blocks, panel_count)
        pick_ref[i] = pick
        own_out[i] = turn(pick, own_ref, i)
        mate_out[i] = turn(pick, mate_ref, i)


def turn_one_kernel(blocks, pick_ref, piece_ref, *refs):
    for i in range(blocks):
        refs[-1][i] = turn(pick_ref[i], piece_ref, i)


def near_kernel(
    sizes, inc, pick_ref, last_ref, below_ref, own_ref, above_ref, *refs
):
    rows, slots, block, blocks, panel_count, swaps = sizes
    keep_ref, send_ref, wide_ref, last_turned = refs[-4:]
    turned = list(refs[:-4]) + [last_turned]
    for i in range(blocks):
        last_turned[i] = turn(pick_ref[i], last_ref, i)
    low, high = ((below_ref, above_ref), (above_ref, below_ref)) if swaps else ((below_ref,), (above_ref,))
    fill_wide(wide_ref, (low, (own_ref,), high), inc, blocks, block)
    for pair in range(blocks // 2):
        sums = []
        for i in (2 * pair, 2 * pair + 1):
            total = None
            for step in range(2 * blocks + 1):
                coefs = []
                for ref in turned:
                    at = step * 2 * rows
                    coefs.append(
                        jnp.concatenate(
                            [ref[i, at : at + rows, :], ref[i, at + rows : at + 2 * rows, :]],
                            axis=1,
                        )
                    )
                start = (i + step) * 2 * block
                term = nt_dot(
                    wide_ref[:, start : start + 2 * block], jnp.concatenate(coefs, axis=0)
                )
                total = term if total is None else total + term
            sums.append(total)
        both = jnp.concatenate(sums, axis=1)
        span = slice(pair * block, (pair + 1) * block)
        keep_ref[:, span] = both[: 2 * inc]
        send_ref[:, span] = both[2 * inc :].astype(BF16)


def near_rows_kernel(sizes, inc, near_ref, coefs_ref, below_ref, own_ref, above_ref, *refs):
    rows, slots, block, blocks, panel_count, swaps = sizes
    keep_ref, send_ref, wide_ref = refs
    low, high = ((below_ref, above_ref), (above_ref, below_ref)) if swaps else ((below_ref,), (above_ref,))
    fill_wide(wide_ref, (low, (own_ref,), high), inc, blocks, block)
    total_blocks = blocks * panel_count
    me = lax.axis_index("panel")
    half = coefs_ref.shape[1]
    for i in range(blocks):
        total = None
        for k in range(slots):
            at = near_ref[i, k] - (me * blocks + i) + blocks
            at = jnp.where(at < 0, at + total_blocks, at)
            at = jnp.where(at >= total_blocks, at - total_blocks, at)
            start = pl.multiple_of(jnp.minimum(at + i, 3 * blocks - 1) * (2 * block), 2 * block)
            coefs = coefs_ref[i, :, k * 2 * block : (k + 1) * 2 * block]
            term = nt_dot(wide_ref[:, pl.ds(start, 2 * block)], coefs)
            total = term if total is None else total + term
        span = slice(i * half, (i + 1) * half)
        keep_ref[:, span] = total[: 2 * inc]
        send_ref[:, span] = total[2 * inc :].astype(BF16)


def in_order(rows_of, bits, rows):
    lanes = rows_of.shape[1]
    lane = lax.broadcasted_iota(jnp.int32, rows_of.shape, 1)
    me = lax.axis_index("inc")
    bit = 1
    while bit < bits:
        shift = bit * rows
        upper = (lane // shift) % 2 == 1
        swapped = jnp.where(
            upper, pltpu.roll(rows_of, shift, 1), pltpu.roll(rows_of, lanes - shift, 1)
        )
        rows_of = jnp.where((me // bit) % 2 == 1, swapped, rows_of)
        bit *= 2
    return rows_of


def base_kernel(
    order, inc, bits, rows, near_ref, rank_ref, field_ref, keep_ref, coupling_ref, target_ref, *refs
):
    count = len(order)
    piece_refs = refs[:count]
    base_ref, place_ref, gathered_ref = refs[count:]
    blocks, _, rank, columns = coupling_ref.shape
    block = target_ref.shape[3]
    size = blocks * rank
    me = lax.axis_index("panel")
    for ref, (step, swap) in zip(piece_refs, order):
        at = lax.bitwise_xor(me, swap) if swap else lax.rem(me + step, count)
        piece = ref[ref.shape[0] - rank :, :]
        for j in range(blocks):
            row = pl.multiple_of(at * size + j * rank, rank)
            gathered_ref[pl.ds(row, rank), :] = piece[:, j * 2 * inc : (j + 1) * 2 * inc]
    block_id = lax.broadcasted_iota(jnp.int32, (rank, columns), 1) // rank
    within = lax.broadcasted_iota(jnp.int32, (rank, columns), 1) % rank
    row = lax.broadcasted_iota(jnp.int32, (rank, columns), 0)
    largest = jnp.maximum(within, row)
    masked = [[], []]
    for i in range(blocks):
        ranks = jnp.zeros((rank, columns), jnp.int32)
        for j in range(columns // rank):
            ranks = jnp.where(block_id == j, rank_ref[i, j], ranks)
        keep = largest < ranks
        for k in range(near_ref.shape[1]):
            keep = keep & (block_id != near_ref[i, k])
        for part in range(2):
            value = coupling_ref[i, part].astype(F32)
            masked[part].append(jnp.where(keep, value, 0.0).astype(BF16))
    masked = jnp.concatenate(masked[0] + masked[1], axis=0)
    both = jnp.dot(masked, gathered_ref[...], preferred_element_type=F32)
    mixed = (both[:size] + times_i_lanes(both[size:], inc)).astype(BF16).astype(F32)
    mixed = jnp.concatenate([mixed, times_i_lanes(mixed, inc)], axis=0).astype(BF16)
    row_block = lax.broadcasted_iota(jnp.int32, (size, block), 0) // rank
    basis = [
        jnp.concatenate([target_ref[i, part] for i in range(blocks)], axis=0).astype(F32)
        for part in range(2)
    ]
    half = block // 2
    high = lax.axis_index("inc") // (lax.axis_size("inc") // 2) == 1
    empty = jnp.zeros((2 * inc, half), F32)
    sent = lax.broadcasted_iota(jnp.int32, (block, 2 * block), 0)
    lane = lax.broadcasted_iota(jnp.int32, (block, 2 * block), 1)
    me_inc, groups = lax.axis_index("inc"), half // rows
    group = (sent // rows) % groups
    if bits > 1:
        group = lax.bitwise_xor(group, lax.bitwise_xor(me_inc, groups))
    else:
        group = group + lax.bitwise_xor(me_inc // groups, 1) * groups
    target = (sent // half) * block + group * rows + sent % rows
    place_ref[...] = jnp.where(lane == target, 1.0, 0.0).astype(BF16)
    for pair in range(blocks // 2):
        own = keep_ref[:, pair * block : (pair + 1) * block]
        if bits > 1:
            own = in_order(own, bits, rows)
        for i in (2 * pair, 2 * pair + 1):
            spread = jnp.concatenate(
                [jnp.where(row_block == i, basis[part], 0.0) for part in range(2)], axis=0
            ).astype(BF16)
            far = tn_dot(mixed, spread)
            span = slice(i * block, (i + 1) * block)
            kept = own[:, (i - 2 * pair) * half : (i - 2 * pair + 1) * half]
            near = jnp.where(
                high, jnp.concatenate([empty, kept], axis=1), jnp.concatenate([kept, empty], axis=1)
            )
            field = jnp.concatenate([field_ref[0][:, span], field_ref[1][:, span]], axis=0)
            base_ref[:, span] = field.astype(F32) * 0.5 + near + far


def final_kernel(base_ref, got_ref, place_ref, out_ref):
    _, inc, panels = out_ref.shape
    block, width = place_ref.shape
    for pair in range(panels // width):
        near = jnp.dot(
            got_ref[:, pair * block : (pair + 1) * block],
            place_ref[...],
            preferred_element_type=F32,
        )
        span = slice(pair * width, (pair + 1) * width)
        result = (base_ref[:, span] + near).astype(BF16)
        out_ref[0, :, span] = result[:inc]
        out_ref[1, :, span] = result[inc:]


def call(kernel, name, out_shape, ins, out_specs, scratch=(), us=1.0, **more):
    return pl.pallas_call(
        kernel,
        out_shape=out_shape,
        in_specs=ins,
        out_specs=out_specs,
        scratch_shapes=list(scratch),
        compiler_params=params(),
        cost_estimate=cost(us),
        name=name,
        **more,
    )


def local(surface_field, near_block, near_index, source_basis, coupling, target_basis, far_rank):
    blocks, rows, slots, _, block = near_block.shape
    _, inc, panels = surface_field.shape
    rank = source_basis.shape[2]
    panel_count = lax.axis_size("panel")
    inc_count = lax.axis_size("inc")
    half = inc_count // 2
    swaps = panel_count == 4
    lines = rows * slots * 2

    def across(x, bit):
        return lax.ppermute(x, "inc", [(i, i ^ bit) for i in range(inc_count)])

    def onward(x, step, swap=0):
        if swap:
            return lax.ppermute(x, "panel", [(i, i ^ swap) for i in range(panel_count)])
        return lax.ppermute(
            x, "panel", [(i, (i - step) % panel_count) for i in range(panel_count)]
        )

    if swaps:
        order = [(0, 0), (0, 1), (0, 3), (0, 2)]
    else:
        order = [(0, 0), (1, 0), (panel_count - 1, 0)]
        order += [(k, 0) for k in range(2, panel_count - 1)]

    other = across(surface_field, half)
    raw = near_block.reshape(blocks * lines, block)
    paired = half == 4 and rows % 16 == 0
    if paired:
        beyond = across(raw, 2)
        mate = across(raw, 1)

    packed, field = call(
        compress_kernel,
        "compress",
        (
            jax.ShapeDtypeStruct((rank, blocks * 2 * inc), BF16),
            jax.ShapeDtypeStruct(surface_field.shape, BF16),
        ),
        [ANY] * 2,
        (VMEM, VMEM),
        [
            pltpu.VMEM(source_basis.shape, BF16),
            pltpu.SemaphoreType.DMA((2,)),
        ],
        us=0.2,
    )(in_hbm(surface_field), in_hbm(source_basis))
    payload, again = call(
        pack_kernel,
        "pack",
        (
            jax.ShapeDtypeStruct((blocks * 4 * inc + rank, block), BF16),
            jax.ShapeDtypeStruct(packed.shape, BF16),
        ),
        [VMEM] * 3,
        (VMEM, VMEM),
        us=100.0,
    )(field, other, packed)
    first = onward(payload, *order[1])
    second = onward(payload, *order[2])
    rest = [onward(again, *which) for which in order[3:]]

    sizes = (rows, slots, block, blocks, panel_count, swaps)
    width = blocks * half * rows
    near_shape = (
        jax.ShapeDtypeStruct((2 * inc, width), F32),
        jax.ShapeDtypeStruct((2 * inc, width), BF16),
    )
    wide = pltpu.VMEM((4 * inc, 3 * blocks * 2 * block), BF16)
    if paired:
        picked = (2 * blocks + 1) * 2 * rows
        shape = jax.ShapeDtypeStruct((blocks, picked, block), BF16)
        pick, own_turned, mate_turned = call(
            functools.partial(turn_first_kernel, sizes),
            "turn_first",
            (jax.ShapeDtypeStruct((blocks, picked, lines), BF16), shape, shape),
            [VMEM] * 3,
            (VMEM,) * 3,
            us=TURN,
        )(near_index, raw, mate)
        last = across(beyond, 1)
        beyond_turned = call(
            functools.partial(turn_one_kernel, blocks),
            "turn_beyond",
            shape,
            [VMEM] * 2,
            VMEM,
            us=TURN2,
        )(pick, beyond)
        keep, send = call(
            functools.partial(near_kernel, sizes, inc),
            "near",
            near_shape,
            [VMEM] * 8,
            (VMEM, VMEM),
            [wide, pltpu.VMEM(shape.shape, BF16)],
        )(pick, last, second, payload, first, own_turned, mate_turned, beyond_turned)
    else:
        coefs = {0: near_block.reshape(blocks, rows, slots * 2 * block)}
        bit = half // 2
        while bit:
            for at in sorted(coefs):
                coefs[at | bit] = across(coefs[at], bit)
            bit //= 2
        me = lax.axis_index("inc") % half
        stacked = jnp.stack([coefs[at] for at in range(half)], axis=1)
        stacked = jnp.take(stacked, jnp.arange(half) ^ me, axis=1)
        stacked = stacked.reshape(blocks, half * rows, slots * 2 * block)
        keep, send = call(
            functools.partial(near_rows_kernel, sizes, inc),
            "near_rows",
            near_shape,
            [SMEM] + [VMEM] * 4,
            (VMEM, VMEM),
            [wide],
        )(near_index, stacked, second, payload, first)
    bits = half if paired else 1
    got = across(send, half)

    base, place = call(
        functools.partial(base_kernel, order, inc, bits, rows),
        "base",
        (
            jax.ShapeDtypeStruct((2 * inc, panels), F32),
            jax.ShapeDtypeStruct((block, 2 * block), BF16),
        ),
        [SMEM] * 2 + [VMEM] * (4 + panel_count),
        (VMEM, VMEM),
        [pltpu.VMEM((panel_count * blocks * rank, 2 * inc), BF16)],
    )(near_index, far_rank, field, keep, coupling, target_basis, packed, first, second, *rest)

    return call(
        final_kernel,
        "final",
        jax.ShapeDtypeStruct((2, inc, panels), BF16),
        [VMEM] * 3,
        VMEM,
    )(base, got, place)


def solution(mesh):
    return jax.shard_map(
        local,
        mesh=mesh,
        in_specs=(
            P(None, "inc", "panel"),
            P("panel", "inc", None, None, None),
            P("panel", None),
            P("panel", None, None, None),
            P("panel", None, None, None),
            P("panel", None, None, None),
            P("panel", None),
        ),
        out_specs=P(None, "inc", "panel"),
        check_vma=False,
    )
```

```python
import functools

import jax
import jax.numpy as jnp
from jax import lax
from jax.experimental import pallas as pl
from jax.experimental.pallas import tpu as pltpu
from jax.sharding import PartitionSpec as P

F32 = jnp.float32
BF16 = jnp.bfloat16
VMEM = pl.BlockSpec(memory_space=pltpu.VMEM)
SMEM = pl.BlockSpec(memory_space=pltpu.SMEM)
ANY = pl.BlockSpec(memory_space=pl.ANY)


TURN = 3.0
TURN2 = 3.0


def params():
    return pltpu.CompilerParams(vmem_limit_bytes=8 * 1024 * 1024)


def cost(us):
    return pl.CostEstimate(flops=int(us * 1e9), bytes_accessed=0, transcendentals=0)


def in_hbm(x):
    return pltpu.with_memory_space_constraint(x, pltpu.HBM)


def nt_dot(left, right):
    return lax.dot_general(left, right, (((1,), (1,)), ((), ())), preferred_element_type=F32)


def tn_dot(left, right):
    return lax.dot_general(left, right, (((0,), (0,)), ((), ())), preferred_element_type=F32)


def times_i(pair_rows, width):
    return jnp.concatenate([-pair_rows[width:], pair_rows[:width]], axis=0)


def times_i_lanes(pair_lanes, width):
    return jnp.concatenate([-pair_lanes[:, width:], pair_lanes[:, :width]], axis=1)


def compress_kernel(field_hbm, basis_hbm, packed_ref, field_ref, basis_ref, sems):
    copies = [
        pltpu.make_async_copy(field_hbm, field_ref, sems.at[0]),
        pltpu.make_async_copy(basis_hbm, basis_ref, sems.at[1]),
    ]
    for copy in copies:
        copy.start()
    for copy in copies:
        copy.wait()
    _, inc, _ = field_ref.shape
    blocks, _, rank, block = basis_ref.shape
    pieces = []
    for j in range(blocks):
        basis = jnp.concatenate([basis_ref[j, 0], basis_ref[j, 1]], axis=0)
        field = jnp.concatenate(
            [field_ref[part][:, j * block : (j + 1) * block] for part in range(2)], axis=0
        )
        both = nt_dot(basis, field)
        pieces.append(both[:rank] + times_i_lanes(both[rank:], inc))
    packed_ref[...] = jnp.concatenate(pieces, axis=1).astype(BF16)


def pack_kernel(own_ref, other_ref, packed_ref, payload_ref, again_ref):
    _, inc, panels = own_ref.shape
    block = payload_ref.shape[1]
    for b in range(panels // block):
        for side, ref in enumerate((own_ref, other_ref)):
            for part in range(2):
                at = ((b * 2 + side) * 2 + part) * inc
                payload_ref[at : at + inc, :] = ref[part][:, b * block : (b + 1) * block]
    payload_ref[4 * inc * (panels // block) :, :] = packed_ref[...]
    again_ref[...] = packed_ref[...]


def fill_wide(wide_ref, window_refs, inc, blocks, block, sides):
    for w, refs in enumerate(window_refs):
        for b in range(blocks):
            at = (w * blocks + b) * 2 * block
            for n, side in enumerate(sides):
                start = (b * 2 + side) * 2 * inc
                piece = refs[0][start : start + 2 * inc, :]
                if len(refs) == 2:
                    odd = lax.rem(lax.axis_index("panel") + lax.axis_index("inc"), 2) == 1
                    piece = jnp.where(odd, refs[1][start : start + 2 * inc, :], piece)
                rows = slice(n * 2 * inc, (n + 1) * 2 * inc)
                wide_ref[rows, at : at + block] = piece
                wide_ref[rows, at + block : at + 2 * block] = times_i(piece, inc)


def pick_matrix(near_ref, i, rows, slots, blocks, panel_count):
    total = blocks * panel_count
    shape = ((2 * blocks + 1) * 2 * rows, rows * slots * 2)
    out = lax.broadcasted_iota(jnp.int32, shape, 0)
    col = lax.broadcasted_iota(jnp.int32, (1, shape[1]), 1)
    slot = (col // 2) % slots
    distance = jnp.zeros((1, shape[1]), jnp.int32)
    for k in range(slots):
        distance = jnp.where(slot == k, near_ref[i : i + 1, k : k + 1], distance)
    distance = distance - (lax.axis_index("panel") * blocks + i) + blocks
    distance = jnp.where(distance < 0, distance + total, distance)
    distance = jnp.where(distance >= total, distance - total, distance)
    source = (distance * 2 + col % 2) * rows + col // (2 * slots)
    return jnp.where(out == source, 1.0, 0.0).astype(BF16)


def turn(pick, piece_ref, i):
    lines = pick.shape[1]
    piece = piece_ref[i * lines : (i + 1) * lines, :]
    return jnp.dot(pick, piece, preferred_element_type=F32).astype(BF16)


def turn_first_kernel(sizes, near_ref, *refs):
    rows, slots, block, blocks, panel_count, swaps = sizes
    own_ref, mate_ref = refs[:2]
    pick_ref, own_out, mate_out = refs[-3:]
    for i in range(blocks):
        pick = pick_matrix(near_ref, i, rows, slots, blocks, panel_count)
        pick_ref[i] = pick
        own_out[i] = turn(pick, own_ref, i)
        mate_out[i] = turn(pick, mate_ref, i)


def turn_one_kernel(blocks, pick_ref, piece_ref, *refs):
    for i in range(blocks):
        refs[-1][i] = turn(pick_ref[i], piece_ref, i)


def near_kernel(
    sizes, inc, pick_ref, last_ref, below_ref, own_ref, above_ref, *refs
):
    rows, slots, block, blocks, panel_count, swaps = sizes
    send_ref, last_turned, wide_ref = refs[-3:]
    turned = list(refs[:-3]) + [last_turned]
    for i in range(blocks):
        last_turned[i] = turn(pick_ref[i], last_ref, i)
    near_sums(sizes, inc, 1, turned, (below_ref, own_ref, above_ref), wide_ref, send_ref)


def near_keep_kernel(sizes, inc, below_ref, own_ref, above_ref, *refs):
    keep_ref, wide_ref = refs[-2:]
    near_sums(sizes, inc, 0, refs[:-2], (below_ref, own_ref, above_ref), wide_ref, keep_ref)


def near_sums(sizes, inc, side, turned, windows, wide_ref, out_ref):
    rows, slots, block, blocks, panel_count, swaps = sizes
    below_ref, own_ref, above_ref = windows
    low, high = ((below_ref, above_ref), (above_ref, below_ref)) if swaps else ((below_ref,), (above_ref,))
    fill_wide(wide_ref, (low, (own_ref,), high), inc, blocks, block, (side,))
    for pair in range(blocks // 2):
        sums = []
        for i in (2 * pair, 2 * pair + 1):
            total = None
            for step in range(2 * blocks + 1):
                coefs = []
                for ref in turned:
                    at = step * 2 * rows
                    coefs.append(
                        jnp.concatenate(
                            [ref[i, at : at + rows, :], ref[i, at + rows : at + 2 * rows, :]],
                            axis=1,
                        )
                    )
                start = (i + step) * 2 * block
                term = nt_dot(
                    wide_ref[:, start : start + 2 * block], jnp.concatenate(coefs, axis=0)
                )
                total = term if total is None else total + term
            sums.append(total)
        span = slice(pair * block, (pair + 1) * block)
        out_ref[:, span] = jnp.concatenate(sums, axis=1).astype(out_ref.dtype)


def near_rows_kernel(sizes, inc, near_ref, coefs_ref, below_ref, own_ref, above_ref, *refs):
    rows, slots, block, blocks, panel_count, swaps = sizes
    keep_ref, send_ref, wide_ref = refs
    low, high = ((below_ref, above_ref), (above_ref, below_ref)) if swaps else ((below_ref,), (above_ref,))
    fill_wide(wide_ref, (low, (own_ref,), high), inc, blocks, block, (0, 1))
    total_blocks = blocks * panel_count
    me = lax.axis_index("panel")
    half = coefs_ref.shape[1]
    for i in range(blocks):
        total = None
        for k in range(slots):
            at = near_ref[i, k] - (me * blocks + i) + blocks
            at = jnp.where(at < 0, at + total_blocks, at)
            at = jnp.where(at >= total_blocks, at - total_blocks, at)
            start = pl.multiple_of(jnp.minimum(at + i, 3 * blocks - 1) * (2 * block), 2 * block)
            coefs = coefs_ref[i, :, k * 2 * block : (k + 1) * 2 * block]
            term = nt_dot(wide_ref[:, pl.ds(start, 2 * block)], coefs)
            total = term if total is None else total + term
        span = slice(i * half, (i + 1) * half)
        keep_ref[:, span] = total[: 2 * inc]
        send_ref[:, span] = total[2 * inc :].astype(BF16)


def in_order(rows_of, bits, rows):
    lanes = rows_of.shape[1]
    lane = lax.broadcasted_iota(jnp.int32, rows_of.shape, 1)
    me = lax.axis_index("inc")
    bit = 1
    while bit < bits:
        shift = bit * rows
        upper = (lane // shift) % 2 == 1
        swapped = jnp.where(
            upper, pltpu.roll(rows_of, shift, 1), pltpu.roll(rows_of, lanes - shift, 1)
        )
        rows_of = jnp.where((me // bit) % 2 == 1, swapped, rows_of)
        bit *= 2
    return rows_of


def base_kernel(
    order, inc, bits, rows, near_ref, rank_ref, field_ref, keep_ref, coupling_ref, target_ref, *refs
):
    count = len(order)
    piece_refs = refs[:count]
    base_ref, place_ref, gathered_ref = refs[count:]
    blocks, _, rank, columns = coupling_ref.shape
    block = target_ref.shape[3]
    size = blocks * rank
    me = lax.axis_index("panel")
    core = lax.rem(lax.axis_index("inc"), 2)
    for ref, (step, even, odd) in zip(piece_refs, order):
        swap = jnp.where(core == 1, odd, even)
        at = lax.bitwise_xor(me, swap) if even else lax.rem(me + step, count)
        piece = ref[ref.shape[0] - rank :, :]
        for j in range(blocks):
            row = pl.multiple_of(at * size + j * rank, rank)
            gathered_ref[pl.ds(row, rank), :] = piece[:, j * 2 * inc : (j + 1) * 2 * inc]
    block_id = lax.broadcasted_iota(jnp.int32, (rank, columns), 1) // rank
    within = lax.broadcasted_iota(jnp.int32, (rank, columns), 1) % rank
    row = lax.broadcasted_iota(jnp.int32, (rank, columns), 0)
    largest = jnp.maximum(within, row)
    masked = [[], []]
    for i in range(blocks):
        ranks = jnp.zeros((rank, columns), jnp.int32)
        for j in range(columns // rank):
            ranks = jnp.where(block_id == j, rank_ref[i, j], ranks)
        keep = largest < ranks
        for k in range(near_ref.shape[1]):
            keep = keep & (block_id != near_ref[i, k])
        for part in range(2):
            value = coupling_ref[i, part].astype(F32)
            masked[part].append(jnp.where(keep, value, 0.0).astype(BF16))
    masked = jnp.concatenate(masked[0] + masked[1], axis=0)
    both = jnp.dot(masked, gathered_ref[...], preferred_element_type=F32)
    mixed = (both[:size] + times_i_lanes(both[size:], inc)).astype(BF16).astype(F32)
    mixed = jnp.concatenate([mixed, times_i_lanes(mixed, inc)], axis=0).astype(BF16)
    row_block = lax.broadcasted_iota(jnp.int32, (size, block), 0) // rank
    basis = [
        jnp.concatenate([target_ref[i, part] for i in range(blocks)], axis=0).astype(F32)
        for part in range(2)
    ]
    half = block // 2
    high = lax.axis_index("inc") // (lax.axis_size("inc") // 2) == 1
    empty = jnp.zeros((2 * inc, half), F32)
    sent = lax.broadcasted_iota(jnp.int32, (block, 2 * block), 0)
    lane = lax.broadcasted_iota(jnp.int32, (block, 2 * block), 1)
    me_inc, groups = lax.axis_index("inc"), half // rows
    group = (sent // rows) % groups
    if bits > 1:
        group = lax.bitwise_xor(group, lax.bitwise_xor(me_inc, groups | 1))
    else:
        group = group + lax.bitwise_xor(me_inc // groups, 1) * groups
    target = (sent // half) * block + group * rows + sent % rows
    place_ref[...] = jnp.where(lane == target, 1.0, 0.0).astype(BF16)
    for pair in range(blocks // 2):
        own = keep_ref[:, pair * block : (pair + 1) * block]
        if bits > 1:
            own = in_order(own, bits, rows)
        for i in (2 * pair, 2 * pair + 1):
            spread = jnp.concatenate(
                [jnp.where(row_block == i, basis[part], 0.0) for part in range(2)], axis=0
            ).astype(BF16)
            far = tn_dot(mixed, spread)
            span = slice(i * block, (i + 1) * block)
            kept = own[:, (i - 2 * pair) * half : (i - 2 * pair + 1) * half]
            near = jnp.where(
                high, jnp.concatenate([empty, kept], axis=1), jnp.concatenate([kept, empty], axis=1)
            )
            field = jnp.concatenate([field_ref[0][:, span], field_ref[1][:, span]], axis=0)
            base_ref[:, span] = field.astype(F32) * 0.5 + near + far


def final_kernel(base_ref, got_ref, place_ref, out_ref):
    _, inc, panels = out_ref.shape
    block, width = place_ref.shape
    for pair in range(panels // width):
        near = jnp.dot(
            got_ref[:, pair * block : (pair + 1) * block],
            place_ref[...],
            preferred_element_type=F32,
        )
        span = slice(pair * width, (pair + 1) * width)
        result = (base_ref[:, span] + near).astype(BF16)
        out_ref[0, :, span] = result[:inc]
        out_ref[1, :, span] = result[inc:]


def call(kernel, name, out_shape, ins, out_specs, scratch=(), us=1.0, **more):
    return pl.pallas_call(
        kernel,
        out_shape=out_shape,
        in_specs=ins,
        out_specs=out_specs,
        scratch_shapes=list(scratch),
        compiler_params=params(),
        cost_estimate=cost(us),
        name=name,
        **more,
    )


def local(surface_field, near_block, near_index, source_basis, coupling, target_basis, far_rank):
    blocks, rows, slots, _, block = near_block.shape
    _, inc, panels = surface_field.shape
    rank = source_basis.shape[2]
    panel_count = lax.axis_size("panel")
    inc_count = lax.axis_size("inc")
    half = inc_count // 2
    swaps = panel_count == 4
    lines = rows * slots * 2

    def across(x, bit):
        return lax.ppermute(x, "inc", [(i, i ^ bit) for i in range(inc_count)])

    def onward(x, step, even=0, odd=0):
        if even:
            pairs = [
                (p * inc_count + i, (p ^ (odd if i % 2 else even)) * inc_count + i)
                for p in range(panel_count)
                for i in range(inc_count)
            ]
            return lax.ppermute(x, ("panel", "inc"), pairs)
        return lax.ppermute(
            x, "panel", [(i, (i - step) % panel_count) for i in range(panel_count)]
        )

    if swaps:
        order = [(0, 0, 0), (0, 1, 3), (0, 3, 1), (0, 2, 2)]
    else:
        order = [(0, 0, 0), (1, 0, 0), (panel_count - 1, 0, 0)]
        order += [(k, 0, 0) for k in range(2, panel_count - 1)]

    partner = half | 1
    other = across(surface_field, partner)
    raw = near_block.reshape(blocks * lines, block)
    paired = half == 4 and rows % 16 == 0
    if paired:
        beyond = across(raw, 2)
        mate = across(raw, 1)

    packed, field = call(
        compress_kernel,
        "compress",
        (
            jax.ShapeDtypeStruct((rank, blocks * 2 * inc), BF16),
            jax.ShapeDtypeStruct(surface_field.shape, BF16),
        ),
        [ANY] * 2,
        (VMEM, VMEM),
        [
            pltpu.VMEM(source_basis.shape, BF16),
            pltpu.SemaphoreType.DMA((2,)),
        ],
        us=0.2,
    )(in_hbm(surface_field), in_hbm(source_basis))
    payload, again = call(
        pack_kernel,
        "pack",
        (
            jax.ShapeDtypeStruct((blocks * 4 * inc + rank, block), BF16),
            jax.ShapeDtypeStruct(packed.shape, BF16),
        ),
        [VMEM] * 3,
        (VMEM, VMEM),
        us=100.0,
    )(field, other, packed)
    first = onward(payload, *order[1])
    second = onward(payload, *order[2])
    rest = [onward(again, *which) for which in order[3:]]

    sizes = (rows, slots, block, blocks, panel_count, swaps)
    width = blocks * half * rows
    near_shape = (
        jax.ShapeDtypeStruct((2 * inc, width), F32),
        jax.ShapeDtypeStruct((2 * inc, width), BF16),
    )
    wide = pltpu.VMEM((4 * inc, 3 * blocks * 2 * block), BF16)
    if paired:
        picked = (2 * blocks + 1) * 2 * rows
        shape = jax.ShapeDtypeStruct((blocks, picked, block), BF16)
        pick, own_turned, mate_turned = call(
            functools.partial(turn_first_kernel, sizes),
            "turn_first",
            (jax.ShapeDtypeStruct((blocks, picked, lines), BF16), shape, shape),
            [VMEM] * 3,
            (VMEM,) * 3,
            us=TURN,
        )(near_index, raw, mate)
        last = across(beyond, 1)
        beyond_turned = call(
            functools.partial(turn_one_kernel, blocks),
            "turn_beyond",
            shape,
            [VMEM] * 2,
            VMEM,
            us=TURN2,
        )(pick, beyond)
        wide = pltpu.VMEM((2 * inc, 3 * blocks * 2 * block), BF16)
        windows = (second, payload, first)
        turned = (own_turned, mate_turned, beyond_turned)
        send, last_turned = call(
            functools.partial(near_kernel, sizes, inc),
            "near_send",
            (near_shape[1], shape),
            [VMEM] * 8,
            (VMEM, VMEM),
            [wide],
        )(pick, last, *windows, *turned)
        keep = call(
            functools.partial(near_keep_kernel, sizes, inc),
            "near_keep",
            near_shape[0],
            [VMEM] * 7,
            VMEM,
            [wide],
        )(*windows, *turned, last_turned)
    else:
        coefs = {0: near_block.reshape(blocks, rows, slots * 2 * block)}
        bit = half // 2
        while bit:
            for at in sorted(coefs):
                coefs[at | bit] = across(coefs[at], bit)
            bit //= 2
        me = lax.axis_index("inc") % half
        stacked = jnp.stack([coefs[at] for at in range(half)], axis=1)
        stacked = jnp.take(stacked, jnp.arange(half) ^ me, axis=1)
        stacked = stacked.reshape(blocks, half * rows, slots * 2 * block)
        keep, send = call(
            functools.partial(near_rows_kernel, sizes, inc),
            "near_rows",
            near_shape,
            [SMEM] + [VMEM] * 4,
            (VMEM, VMEM),
            [wide],
        )(near_index, stacked, second, payload, first)
    bits = half if paired else 1
    got = across(send, partner)

    base, place = call(
        functools.partial(base_kernel, order, inc, bits, rows),
        "base",
        (
            jax.ShapeDtypeStruct((2 * inc, panels), F32),
            jax.ShapeDtypeStruct((block, 2 * block), BF16),
        ),
        [SMEM] * 2 + [VMEM] * (4 + panel_count),
        (VMEM, VMEM),
        [pltpu.VMEM((panel_count * blocks * rank, 2 * inc), BF16)],
    )(near_index, far_rank, field, keep, coupling, target_basis, packed, first, second, *rest)

    return call(
        final_kernel,
        "final",
        jax.ShapeDtypeStruct((2, inc, panels), BF16),
        [VMEM] * 3,
        VMEM,
    )(base, got, place)


def solution(mesh):
    return jax.shard_map(
        local,
        mesh=mesh,
        in_specs=(
            P(None, "inc", "panel"),
            P("panel", "inc", None, None, None),
            P("panel", None),
            P("panel", None, None, None),
            P("panel", None, None, None),
            P("panel", None, None, None),
            P("panel", None),
        ),
        out_specs=P(None, "inc", "panel"),
        check_vma=False,
    )
```

```python
import functools

import jax
import jax.numpy as jnp
from jax import lax
from jax.experimental import pallas as pl
from jax.experimental.pallas import tpu as pltpu
from jax.sharding import PartitionSpec as P

F32 = jnp.float32
BF16 = jnp.bfloat16
VMEM = pl.BlockSpec(memory_space=pltpu.VMEM)
SMEM = pl.BlockSpec(memory_space=pltpu.SMEM)
ANY = pl.BlockSpec(memory_space=pl.ANY)


TURN = 3.0
TURN2 = 3.0
EARLY = 1.0


def params():
    return pltpu.CompilerParams(vmem_limit_bytes=8 * 1024 * 1024)


def cost(us):
    return pl.CostEstimate(flops=int(us * 1e9), bytes_accessed=0, transcendentals=0)


def in_hbm(x):
    return pltpu.with_memory_space_constraint(x, pltpu.HBM)


def nt_dot(left, right):
    return lax.dot_general(left, right, (((1,), (1,)), ((), ())), preferred_element_type=F32)


def tn_dot(left, right):
    return lax.dot_general(left, right, (((0,), (0,)), ((), ())), preferred_element_type=F32)


def times_i(pair_rows, width):
    return jnp.concatenate([-pair_rows[width:], pair_rows[:width]], axis=0)


def times_i_lanes(pair_lanes, width):
    return jnp.concatenate([-pair_lanes[:, width:], pair_lanes[:, :width]], axis=1)


def compress_kernel(field_hbm, basis_hbm, packed_ref, field_ref, basis_ref, sems):
    copies = [
        pltpu.make_async_copy(field_hbm, field_ref, sems.at[0]),
        pltpu.make_async_copy(basis_hbm, basis_ref, sems.at[1]),
    ]
    for copy in copies:
        copy.start()
    for copy in copies:
        copy.wait()
    _, inc, _ = field_ref.shape
    blocks, _, rank, block = basis_ref.shape
    pieces = []
    for j in range(blocks):
        basis = jnp.concatenate([basis_ref[j, 0], basis_ref[j, 1]], axis=0)
        field = jnp.concatenate(
            [field_ref[part][:, j * block : (j + 1) * block] for part in range(2)], axis=0
        )
        both = nt_dot(basis, field)
        pieces.append(both[:rank] + times_i_lanes(both[rank:], inc))
    packed_ref[...] = jnp.concatenate(pieces, axis=1).astype(BF16)


def pack_kernel(own_ref, other_ref, packed_ref, payload_ref, again_ref):
    _, inc, panels = own_ref.shape
    block = payload_ref.shape[1]
    for b in range(panels // block):
        for side, ref in enumerate((own_ref, other_ref)):
            for part in range(2):
                at = ((b * 2 + side) * 2 + part) * inc
                payload_ref[at : at + inc, :] = ref[part][:, b * block : (b + 1) * block]
    payload_ref[4 * inc * (panels // block) :, :] = packed_ref[...]
    again_ref[...] = packed_ref[...]


def fill_wide(wide_ref, window_refs, inc, blocks, block, sides):
    for w, refs in enumerate(window_refs):
        for b in range(blocks):
            at = (w * blocks + b) * 2 * block
            for n, side in enumerate(sides):
                start = (b * 2 + side) * 2 * inc
                piece = refs[0][start : start + 2 * inc, :]
                if len(refs) == 2:
                    odd = lax.rem(lax.axis_index("panel") + lax.axis_index("inc"), 2) == 1
                    piece = jnp.where(odd, refs[1][start : start + 2 * inc, :], piece)
                rows = slice(n * 2 * inc, (n + 1) * 2 * inc)
                wide_ref[rows, at : at + block] = piece
                wide_ref[rows, at + block : at + 2 * block] = times_i(piece, inc)


def pick_matrix(near_ref, i, rows, slots, blocks, panel_count):
    total = blocks * panel_count
    shape = ((2 * blocks + 1) * 2 * rows, rows * slots * 2)
    out = lax.broadcasted_iota(jnp.int32, shape, 0)
    col = lax.broadcasted_iota(jnp.int32, (1, shape[1]), 1)
    slot = (col // 2) % slots
    distance = jnp.zeros((1, shape[1]), jnp.int32)
    for k in range(slots):
        distance = jnp.where(slot == k, near_ref[i : i + 1, k : k + 1], distance)
    distance = distance - (lax.axis_index("panel") * blocks + i) + blocks
    distance = jnp.where(distance < 0, distance + total, distance)
    distance = jnp.where(distance >= total, distance - total, distance)
    source = (distance * 2 + col % 2) * rows + col // (2 * slots)
    return jnp.where(out == source, 1.0, 0.0).astype(BF16)


def turn(pick, piece_ref, i):
    lines = pick.shape[1]
    piece = piece_ref[i * lines : (i + 1) * lines, :]
    return jnp.dot(pick, piece, preferred_element_type=F32).astype(BF16)


def turn_first_kernel(sizes, near_ref, *refs):
    rows, slots, block, blocks, panel_count, swaps = sizes
    own_ref, mate_ref = refs[:2]
    pick_ref, own_out, mate_out = refs[-3:]
    for i in range(blocks):
        pick = pick_matrix(near_ref, i, rows, slots, blocks, panel_count)
        pick_ref[i] = pick
        own_out[i] = turn(pick, own_ref, i)
        mate_out[i] = turn(pick, mate_ref, i)


def turn_one_kernel(blocks, pick_ref, piece_ref, *refs):
    for i in range(blocks):
        refs[-1][i] = turn(pick_ref[i], piece_ref, i)


def near_early_kernel(sizes, inc, below_ref, own_ref, above_ref, *refs):
    blocks, block = sizes[3], sizes[2]
    part_ref, wide_ref = refs[-2:]
    fill_windows(sizes, inc, 1, (below_ref, own_ref, above_ref), wide_ref)
    sums = near_sums(sizes, refs[:-2], wide_ref)
    width = part_ref.shape[1] // blocks
    for i in range(blocks):
        part_ref[:, i * width : i * width + sums[i].shape[1]] = sums[i]


def near_last_kernel(sizes, pick_ref, last_ref, wide_ref, part_ref, send_ref, last_turned):
    rows, slots, block, blocks, panel_count, swaps = sizes
    for i in range(blocks):
        last_turned[i] = turn(pick_ref[i], last_ref, i)
    sums = near_sums(sizes, [last_turned], wide_ref)
    width = part_ref.shape[1] // blocks
    for pair in range(blocks // 2):
        both = []
        for i in (2 * pair, 2 * pair + 1):
            both += [part_ref[:, i * width : (i + 1) * width - rows], sums[i]]
        span = slice(pair * block, (pair + 1) * block)
        send_ref[:, span] = jnp.concatenate(both, axis=1).astype(BF16)


def near_keep_kernel(sizes, inc, below_ref, own_ref, above_ref, *refs):
    block, blocks = sizes[2], sizes[3]
    keep_ref, wide_ref = refs[-2:]
    fill_windows(sizes, inc, 0, (below_ref, own_ref, above_ref), wide_ref)
    sums = near_sums(sizes, refs[:-2], wide_ref)
    for pair in range(blocks // 2):
        span = slice(pair * block, (pair + 1) * block)
        keep_ref[:, span] = jnp.concatenate(sums[2 * pair : 2 * pair + 2], axis=1)


def fill_windows(sizes, inc, side, windows, wide_ref):
    rows, slots, block, blocks, panel_count, swaps = sizes
    below_ref, own_ref, above_ref = windows
    low, high = ((below_ref, above_ref), (above_ref, below_ref)) if swaps else ((below_ref,), (above_ref,))
    fill_wide(wide_ref, (low, (own_ref,), high), inc, blocks, block, (side,))


def near_sums(sizes, turned, wide_ref):
    rows, slots, block, blocks, panel_count, swaps = sizes
    sums = []
    for i in range(blocks):
        total = None
        for step in range(2 * blocks + 1):
            at = step * 2 * rows
            coefs = [
                jnp.concatenate(
                    [ref[i, at : at + rows, :], ref[i, at + rows : at + 2 * rows, :]], axis=1
                )
                for ref in turned
            ]
            coefs = coefs[0] if len(coefs) == 1 else jnp.concatenate(coefs, axis=0)
            start = (i + step) * 2 * block
            term = nt_dot(wide_ref[:, start : start + 2 * block], coefs)
            total = term if total is None else total + term
        sums.append(total)
    return sums


def near_rows_kernel(sizes, inc, near_ref, coefs_ref, below_ref, own_ref, above_ref, *refs):
    rows, slots, block, blocks, panel_count, swaps = sizes
    keep_ref, send_ref, wide_ref = refs
    low, high = ((below_ref, above_ref), (above_ref, below_ref)) if swaps else ((below_ref,), (above_ref,))
    fill_wide(wide_ref, (low, (own_ref,), high), inc, blocks, block, (0, 1))
    total_blocks = blocks * panel_count
    me = lax.axis_index("panel")
    half = coefs_ref.shape[1]
    for i in range(blocks):
        total = None
        for k in range(slots):
            at = near_ref[i, k] - (me * blocks + i) + blocks
            at = jnp.where(at < 0, at + total_blocks, at)
            at = jnp.where(at >= total_blocks, at - total_blocks, at)
            start = pl.multiple_of(jnp.minimum(at + i, 3 * blocks - 1) * (2 * block), 2 * block)
            coefs = coefs_ref[i, :, k * 2 * block : (k + 1) * 2 * block]
            term = nt_dot(wide_ref[:, pl.ds(start, 2 * block)], coefs)
            total = term if total is None else total + term
        span = slice(i * half, (i + 1) * half)
        keep_ref[:, span] = total[: 2 * inc]
        send_ref[:, span] = total[2 * inc :].astype(BF16)


def in_order(rows_of, bits, rows):
    lanes = rows_of.shape[1]
    lane = lax.broadcasted_iota(jnp.int32, rows_of.shape, 1)
    me = lax.axis_index("inc")
    bit = 1
    while bit < bits:
        shift = bit * rows
        upper = (lane // shift) % 2 == 1
        swapped = jnp.where(
            upper, pltpu.roll(rows_of, shift, 1), pltpu.roll(rows_of, lanes - shift, 1)
        )
        rows_of = jnp.where((me // bit) % 2 == 1, swapped, rows_of)
        bit *= 2
    return rows_of


def base_kernel(
    order, inc, bits, rows, near_ref, rank_ref, field_ref, keep_ref, coupling_ref, target_ref, *refs
):
    count = len(order)
    piece_refs = refs[:count]
    base_ref, place_ref, gathered_ref = refs[count:]
    blocks, _, rank, columns = coupling_ref.shape
    block = target_ref.shape[3]
    size = blocks * rank
    me = lax.axis_index("panel")
    core = lax.rem(lax.axis_index("inc"), 2)
    for ref, (step, even, odd) in zip(piece_refs, order):
        swap = jnp.where(core == 1, odd, even)
        at = lax.bitwise_xor(me, swap) if even else lax.rem(me + step, count)
        piece = ref[ref.shape[0] - rank :, :]
        for j in range(blocks):
            row = pl.multiple_of(at * size + j * rank, rank)
            gathered_ref[pl.ds(row, rank), :] = piece[:, j * 2 * inc : (j + 1) * 2 * inc]
    block_id = lax.broadcasted_iota(jnp.int32, (rank, columns), 1) // rank
    within = lax.broadcasted_iota(jnp.int32, (rank, columns), 1) % rank
    row = lax.broadcasted_iota(jnp.int32, (rank, columns), 0)
    largest = jnp.maximum(within, row)
    masked = [[], []]
    for i in range(blocks):
        ranks = jnp.zeros((rank, columns), jnp.int32)
        for j in range(columns // rank):
            ranks = jnp.where(block_id == j, rank_ref[i, j], ranks)
        keep = largest < ranks
        for k in range(near_ref.shape[1]):
            keep = keep & (block_id != near_ref[i, k])
        for part in range(2):
            value = coupling_ref[i, part].astype(F32)
            masked[part].append(jnp.where(keep, value, 0.0).astype(BF16))
    masked = jnp.concatenate(masked[0] + masked[1], axis=0)
    both = jnp.dot(masked, gathered_ref[...], preferred_element_type=F32)
    mixed = (both[:size] + times_i_lanes(both[size:], inc)).astype(BF16).astype(F32)
    mixed = jnp.concatenate([mixed, times_i_lanes(mixed, inc)], axis=0).astype(BF16)
    row_block = lax.broadcasted_iota(jnp.int32, (size, block), 0) // rank
    basis = [
        jnp.concatenate([target_ref[i, part] for i in range(blocks)], axis=0).astype(F32)
        for part in range(2)
    ]
    half = block // 2
    high = lax.axis_index("inc") // (lax.axis_size("inc") // 2) == 1
    empty = jnp.zeros((2 * inc, half), F32)
    sent = lax.broadcasted_iota(jnp.int32, (block, 2 * block), 0)
    lane = lax.broadcasted_iota(jnp.int32, (block, 2 * block), 1)
    me_inc, groups = lax.axis_index("inc"), half // rows
    group = (sent // rows) % groups
    if bits > 1:
        group = lax.bitwise_xor(group, lax.bitwise_xor(me_inc, groups | 1))
    else:
        group = group + lax.bitwise_xor(me_inc // groups, 1) * groups
    target = (sent // half) * block + group * rows + sent % rows
    place_ref[...] = jnp.where(lane == target, 1.0, 0.0).astype(BF16)
    for pair in range(blocks // 2):
        own = keep_ref[:, pair * block : (pair + 1) * block]
        if bits > 1:
            own = in_order(own, bits, rows)
        for i in (2 * pair, 2 * pair + 1):
            spread = jnp.concatenate(
                [jnp.where(row_block == i, basis[part], 0.0) for part in range(2)], axis=0
            ).astype(BF16)
            far = tn_dot(mixed, spread)
            span = slice(i * block, (i + 1) * block)
            kept = own[:, (i - 2 * pair) * half : (i - 2 * pair + 1) * half]
            near = jnp.where(
                high, jnp.concatenate([empty, kept], axis=1), jnp.concatenate([kept, empty], axis=1)
            )
            field = jnp.concatenate([field_ref[0][:, span], field_ref[1][:, span]], axis=0)
            base_ref[:, span] = field.astype(F32) * 0.5 + near + far


def final_kernel(base_ref, got_ref, place_ref, out_ref):
    _, inc, panels = out_ref.shape
    block, width = place_ref.shape
    for pair in range(panels // width):
        near = jnp.dot(
            got_ref[:, pair * block : (pair + 1) * block],
            place_ref[...],
            preferred_element_type=F32,
        )
        span = slice(pair * width, (pair + 1) * width)
        result = (base_ref[:, span] + near).astype(BF16)
        out_ref[0, :, span] = result[:inc]
        out_ref[1, :, span] = result[inc:]


def call(kernel, name, out_shape, ins, out_specs, scratch=(), us=1.0, **more):
    return pl.pallas_call(
        kernel,
        out_shape=out_shape,
        in_specs=ins,
        out_specs=out_specs,
        scratch_shapes=list(scratch),
        compiler_params=params(),
        cost_estimate=cost(us),
        name=name,
        **more,
    )


def local(surface_field, near_block, near_index, source_basis, coupling, target_basis, far_rank):
    blocks, rows, slots, _, block = near_block.shape
    _, inc, panels = surface_field.shape
    rank = source_basis.shape[2]
    panel_count = lax.axis_size("panel")
    inc_count = lax.axis_size("inc")
    half = inc_count // 2
    swaps = panel_count == 4
    lines = rows * slots * 2

    def across(x, bit):
        return lax.ppermute(x, "inc", [(i, i ^ bit) for i in range(inc_count)])

    def onward(x, step, even=0, odd=0):
        if even:
            pairs = [
                (p * inc_count + i, (p ^ (odd if i % 2 else even)) * inc_count + i)
                for p in range(panel_count)
                for i in range(inc_count)
            ]
            return lax.ppermute(x, ("panel", "inc"), pairs)
        return lax.ppermute(
            x, "panel", [(i, (i - step) % panel_count) for i in range(panel_count)]
        )

    if swaps:
        order = [(0, 0, 0), (0, 1, 3), (0, 3, 1), (0, 2, 2)]
    else:
        order = [(0, 0, 0), (1, 0, 0), (panel_count - 1, 0, 0)]
        order += [(k, 0, 0) for k in range(2, panel_count - 1)]

    partner = half | 1
    other = across(surface_field, partner)
    raw = near_block.reshape(blocks * lines, block)
    paired = half == 4 and rows % 16 == 0
    if paired:
        beyond = across(raw, 2)
        mate = across(raw, 1)

    packed, field = call(
        compress_kernel,
        "compress",
        (
            jax.ShapeDtypeStruct((rank, blocks * 2 * inc), BF16),
            jax.ShapeDtypeStruct(surface_field.shape, BF16),
        ),
        [ANY] * 2,
        (VMEM, VMEM),
        [
            pltpu.VMEM(source_basis.shape, BF16),
            pltpu.SemaphoreType.DMA((2,)),
        ],
        us=0.2,
    )(in_hbm(surface_field), in_hbm(source_basis))
    payload, again = call(
        pack_kernel,
        "pack",
        (
            jax.ShapeDtypeStruct((blocks * 4 * inc + rank, block), BF16),
            jax.ShapeDtypeStruct(packed.shape, BF16),
        ),
        [VMEM] * 3,
        (VMEM, VMEM),
        us=100.0,
    )(field, other, packed)
    first = onward(payload, *order[1])
    second = onward(payload, *order[2])
    rest = [onward(again, *which) for which in order[3:]]

    sizes = (rows, slots, block, blocks, panel_count, swaps)
    width = blocks * half * rows
    near_shape = (
        jax.ShapeDtypeStruct((2 * inc, width), F32),
        jax.ShapeDtypeStruct((2 * inc, width), BF16),
    )
    wide = pltpu.VMEM((4 * inc, 3 * blocks * 2 * block), BF16)
    if paired:
        picked = (2 * blocks + 1) * 2 * rows
        shape = jax.ShapeDtypeStruct((blocks, picked, block), BF16)
        pick, own_turned, mate_turned = call(
            functools.partial(turn_first_kernel, sizes),
            "turn_first",
            (jax.ShapeDtypeStruct((blocks, picked, lines), BF16), shape, shape),
            [VMEM] * 3,
            (VMEM,) * 3,
            us=TURN,
        )(near_index, raw, mate)
        last = across(beyond, 1)
        beyond_turned = call(
            functools.partial(turn_one_kernel, blocks),
            "turn_beyond",
            shape,
            [VMEM] * 2,
            VMEM,
            us=TURN2,
        )(pick, beyond)
        wide = pltpu.VMEM((2 * inc, 3 * blocks * 2 * block), BF16)
        windows = (second, payload, first)
        turned = (own_turned, mate_turned, beyond_turned)
        part, filled = call(
            functools.partial(near_early_kernel, sizes, inc),
            "near_early",
            (near_shape[0], jax.ShapeDtypeStruct(wide.shape, BF16)),
            [VMEM] * 6,
            (VMEM, VMEM),
            us=EARLY,
        )(*windows, *turned)
        send, last_turned = call(
            functools.partial(near_last_kernel, sizes),
            "near_last",
            (near_shape[1], shape),
            [VMEM] * 4,
            (VMEM, VMEM),
        )(pick, last, filled, part)
        keep = call(
            functools.partial(near_keep_kernel, sizes, inc),
            "near_keep",
            near_shape[0],
            [VMEM] * 7,
            VMEM,
            [wide],
        )(*windows, *turned, last_turned)
    else:
        coefs = {0: near_block.reshape(blocks, rows, slots * 2 * block)}
        bit = half // 2
        while bit:
            for at in sorted(coefs):
                coefs[at | bit] = across(coefs[at], bit)
            bit //= 2
        me = lax.axis_index("inc") % half
        stacked = jnp.stack([coefs[at] for at in range(half)], axis=1)
        stacked = jnp.take(stacked, jnp.arange(half) ^ me, axis=1)
        stacked = stacked.reshape(blocks, half * rows, slots * 2 * block)
        keep, send = call(
            functools.partial(near_rows_kernel, sizes, inc),
            "near_rows",
            near_shape,
            [SMEM] + [VMEM] * 4,
            (VMEM, VMEM),
            [wide],
        )(near_index, stacked, second, payload, first)
    bits = half if paired else 1
    got = across(send, partner)

    base, place = call(
        functools.partial(base_kernel, order, inc, bits, rows),
        "base",
        (
            jax.ShapeDtypeStruct((2 * inc, panels), F32),
            jax.ShapeDtypeStruct((block, 2 * block), BF16),
        ),
        [SMEM] * 2 + [VMEM] * (4 + panel_count),
        (VMEM, VMEM),
        [pltpu.VMEM((panel_count * blocks * rank, 2 * inc), BF16)],
    )(near_index, far_rank, field, keep, coupling, target_basis, packed, first, second, *rest)

    return call(
        final_kernel,
        "final",
        jax.ShapeDtypeStruct((2, inc, panels), BF16),
        [VMEM] * 3,
        VMEM,
    )(base, got, place)


def solution(mesh):
    return jax.shard_map(
        local,
        mesh=mesh,
        in_specs=(
            P(None, "inc", "panel"),
            P("panel", "inc", None, None, None),
            P("panel", None),
            P("panel", None, None, None),
            P("panel", None, None, None),
            P("panel", None, None, None),
            P("panel", None),
        ),
        out_specs=P(None, "inc", "panel"),
        check_vma=False,
    )
```

```python
import functools

import jax
import jax.numpy as jnp
from jax import lax
from jax.experimental import pallas as pl
from jax.experimental.pallas import tpu as pltpu
from jax.sharding import PartitionSpec as P

F32 = jnp.float32
BF16 = jnp.bfloat16
VMEM = pl.BlockSpec(memory_space=pltpu.VMEM)
SMEM = pl.BlockSpec(memory_space=pltpu.SMEM)
ANY = pl.BlockSpec(memory_space=pl.ANY)


TURN = 3.0
TURN2 = 3.0
EARLY = 1.0


def params():
    return pltpu.CompilerParams(vmem_limit_bytes=8 * 1024 * 1024)


def cost(us):
    return pl.CostEstimate(flops=int(us * 1e9), bytes_accessed=0, transcendentals=0)


def in_hbm(x):
    return pltpu.with_memory_space_constraint(x, pltpu.HBM)


def token_kernel(in_ref, out_ref):
    out_ref[...] = jnp.zeros(out_ref.shape, F32)


def stage_kernel(in_ref, token_ref, out_ref):
    out_ref[...] = in_ref[...]


def nt_dot(left, right):
    return lax.dot_general(left, right, (((1,), (1,)), ((), ())), preferred_element_type=F32)


def tn_dot(left, right):
    return lax.dot_general(left, right, (((0,), (0,)), ((), ())), preferred_element_type=F32)


def times_i(pair_rows, width):
    return jnp.concatenate([-pair_rows[width:], pair_rows[:width]], axis=0)


def times_i_lanes(pair_lanes, width):
    return jnp.concatenate([-pair_lanes[:, width:], pair_lanes[:, :width]], axis=1)


def compress_kernel(field_hbm, basis_hbm, packed_ref, field_ref, basis_ref, sems):
    copies = [
        pltpu.make_async_copy(field_hbm, field_ref, sems.at[0]),
        pltpu.make_async_copy(basis_hbm, basis_ref, sems.at[1]),
    ]
    for copy in copies:
        copy.start()
    for copy in copies:
        copy.wait()
    _, inc, _ = field_ref.shape
    blocks, _, rank, block = basis_ref.shape
    pieces = []
    for j in range(blocks):
        basis = jnp.concatenate([basis_ref[j, 0], basis_ref[j, 1]], axis=0)
        field = jnp.concatenate(
            [field_ref[part][:, j * block : (j + 1) * block] for part in range(2)], axis=0
        )
        both = nt_dot(basis, field)
        pieces.append(both[:rank] + times_i_lanes(both[rank:], inc))
    packed_ref[...] = jnp.concatenate(pieces, axis=1).astype(BF16)


def pack_kernel(own_ref, other_ref, packed_ref, payload_ref, again_ref):
    _, inc, panels = own_ref.shape
    block = payload_ref.shape[1]
    for b in range(panels // block):
        for side, ref in enumerate((own_ref, other_ref)):
            for part in range(2):
                at = ((b * 2 + side) * 2 + part) * inc
                payload_ref[at : at + inc, :] = ref[part][:, b * block : (b + 1) * block]
    payload_ref[4 * inc * (panels // block) :, :] = packed_ref[...]
    again_ref[...] = packed_ref[...]


def fill_wide(wide_ref, window_refs, inc, blocks, block, sides):
    for w, refs in enumerate(window_refs):
        for b in range(blocks):
            at = (w * blocks + b) * 2 * block
            for n, side in enumerate(sides):
                start = (b * 2 + side) * 2 * inc
                piece = refs[0][start : start + 2 * inc, :]
                if len(refs) == 2:
                    odd = lax.rem(lax.axis_index("panel") + lax.axis_index("inc"), 2) == 1
                    piece = jnp.where(odd, refs[1][start : start + 2 * inc, :], piece)
                rows = slice(n * 2 * inc, (n + 1) * 2 * inc)
                wide_ref[rows, at : at + block] = piece
                wide_ref[rows, at + block : at + 2 * block] = times_i(piece, inc)


def pick_matrix(near_ref, i, rows, slots, blocks, panel_count):
    total = blocks * panel_count
    shape = ((2 * blocks + 1) * 2 * rows, rows * slots * 2)
    out = lax.broadcasted_iota(jnp.int32, shape, 0)
    col = lax.broadcasted_iota(jnp.int32, (1, shape[1]), 1)
    slot = (col // 2) % slots
    distance = jnp.zeros((1, shape[1]), jnp.int32)
    for k in range(slots):
        distance = jnp.where(slot == k, near_ref[i : i + 1, k : k + 1], distance)
    distance = distance - (lax.axis_index("panel") * blocks + i) + blocks
    distance = jnp.where(distance < 0, distance + total, distance)
    distance = jnp.where(distance >= total, distance - total, distance)
    source = (distance * 2 + col % 2) * rows + col // (2 * slots)
    return jnp.where(out == source, 1.0, 0.0).astype(BF16)


def turn(pick, piece_ref, i):
    lines = pick.shape[1]
    piece = piece_ref[i * lines : (i + 1) * lines, :]
    return jnp.dot(pick, piece, preferred_element_type=F32).astype(BF16)


def turn_first_kernel(sizes, near_ref, *refs):
    rows, slots, block, blocks, panel_count, swaps = sizes
    own_ref, mate_ref = refs[:2]
    pick_ref, own_out, mate_out = refs[-3:]
    for i in range(blocks):
        pick = pick_matrix(near_ref, i, rows, slots, blocks, panel_count)
        pick_ref[i] = pick
        own_out[i] = turn(pick, own_ref, i)
        mate_out[i] = turn(pick, mate_ref, i)


def turn_one_kernel(blocks, pick_ref, piece_ref, *refs):
    for i in range(blocks):
        refs[-1][i] = turn(pick_ref[i], piece_ref, i)


def near_early_kernel(sizes, inc, below_ref, own_ref, above_ref, *refs):
    blocks, block = sizes[3], sizes[2]
    part_ref, wide_ref = refs[-2:]
    fill_windows(sizes, inc, 1, (below_ref, own_ref, above_ref), wide_ref)
    sums = near_sums(sizes, refs[:-2], wide_ref)
    width = part_ref.shape[1] // blocks
    for i in range(blocks):
        part_ref[:, i * width : i * width + sums[i].shape[1]] = sums[i]


def near_last_kernel(sizes, pick_ref, last_ref, wide_ref, part_ref, send_ref, last_turned):
    rows, slots, block, blocks, panel_count, swaps = sizes
    for i in range(blocks):
        last_turned[i] = turn(pick_ref[i], last_ref, i)
    sums = near_sums(sizes, [last_turned], wide_ref)
    width = part_ref.shape[1] // blocks
    for pair in range(blocks // 2):
        both = []
        for i in (2 * pair, 2 * pair + 1):
            both += [part_ref[:, i * width : (i + 1) * width - rows], sums[i]]
        span = slice(pair * block, (pair + 1) * block)
        send_ref[:, span] = jnp.concatenate(both, axis=1).astype(BF16)


def near_keep_kernel(sizes, inc, below_ref, own_ref, above_ref, *refs):
    block, blocks = sizes[2], sizes[3]
    keep_ref, wide_ref = refs[-2:]
    fill_windows(sizes, inc, 0, (below_ref, own_ref, above_ref), wide_ref)
    sums = near_sums(sizes, refs[:-2], wide_ref)
    for pair in range(blocks // 2):
        span = slice(pair * block, (pair + 1) * block)
        keep_ref[:, span] = jnp.concatenate(sums[2 * pair : 2 * pair + 2], axis=1)


def fill_windows(sizes, inc, side, windows, wide_ref):
    rows, slots, block, blocks, panel_count, swaps = sizes
    below_ref, own_ref, above_ref = windows
    low, high = ((below_ref, above_ref), (above_ref, below_ref)) if swaps else ((below_ref,), (above_ref,))
    fill_wide(wide_ref, (low, (own_ref,), high), inc, blocks, block, (side,))


def near_sums(sizes, turned, wide_ref):
    rows, slots, block, blocks, panel_count, swaps = sizes
    sums = []
    for i in range(blocks):
        total = None
        for step in range(2 * blocks + 1):
            at = step * 2 * rows
            coefs = [
                jnp.concatenate(
                    [ref[i, at : at + rows, :], ref[i, at + rows : at + 2 * rows, :]], axis=1
                )
                for ref in turned
            ]
            coefs = coefs[0] if len(coefs) == 1 else jnp.concatenate(coefs, axis=0)
            start = (i + step) * 2 * block
            term = nt_dot(wide_ref[:, start : start + 2 * block], coefs)
            total = term if total is None else total + term
        sums.append(total)
    return sums


def near_rows_kernel(sizes, inc, near_ref, coefs_ref, below_ref, own_ref, above_ref, *refs):
    rows, slots, block, blocks, panel_count, swaps = sizes
    keep_ref, send_ref, wide_ref = refs
    low, high = ((below_ref, above_ref), (above_ref, below_ref)) if swaps else ((below_ref,), (above_ref,))
    fill_wide(wide_ref, (low, (own_ref,), high), inc, blocks, block, (0, 1))
    total_blocks = blocks * panel_count
    me = lax.axis_index("panel")
    half = coefs_ref.shape[1]
    for i in range(blocks):
        total = None
        for k in range(slots):
            at = near_ref[i, k] - (me * blocks + i) + blocks
            at = jnp.where(at < 0, at + total_blocks, at)
            at = jnp.where(at >= total_blocks, at - total_blocks, at)
            start = pl.multiple_of(jnp.minimum(at + i, 3 * blocks - 1) * (2 * block), 2 * block)
            coefs = coefs_ref[i, :, k * 2 * block : (k + 1) * 2 * block]
            term = nt_dot(wide_ref[:, pl.ds(start, 2 * block)], coefs)
            total = term if total is None else total + term
        span = slice(i * half, (i + 1) * half)
        keep_ref[:, span] = total[: 2 * inc]
        send_ref[:, span] = total[2 * inc :].astype(BF16)


def in_order(rows_of, bits, rows):
    lanes = rows_of.shape[1]
    lane = lax.broadcasted_iota(jnp.int32, rows_of.shape, 1)
    me = lax.axis_index("inc")
    bit = 1
    while bit < bits:
        shift = bit * rows
        upper = (lane // shift) % 2 == 1
        swapped = jnp.where(
            upper, pltpu.roll(rows_of, shift, 1), pltpu.roll(rows_of, lanes - shift, 1)
        )
        rows_of = jnp.where((me // bit) % 2 == 1, swapped, rows_of)
        bit *= 2
    return rows_of


def base_kernel(
    order, inc, bits, rows, near_ref, rank_ref, field_ref, keep_ref, coupling_ref, target_ref, *refs
):
    count = len(order)
    piece_refs = refs[:count]
    base_ref, place_ref, gathered_ref = refs[count:]
    blocks, _, rank, columns = coupling_ref.shape
    block = target_ref.shape[3]
    size = blocks * rank
    me = lax.axis_index("panel")
    core = lax.rem(lax.axis_index("inc"), 2)
    for ref, (step, even, odd) in zip(piece_refs, order):
        swap = jnp.where(core == 1, odd, even)
        at = lax.bitwise_xor(me, swap) if even else lax.rem(me + step, count)
        piece = ref[ref.shape[0] - rank :, :]
        for j in range(blocks):
            row = pl.multiple_of(at * size + j * rank, rank)
            gathered_ref[pl.ds(row, rank), :] = piece[:, j * 2 * inc : (j + 1) * 2 * inc]
    block_id = lax.broadcasted_iota(jnp.int32, (rank, columns), 1) // rank
    within = lax.broadcasted_iota(jnp.int32, (rank, columns), 1) % rank
    row = lax.broadcasted_iota(jnp.int32, (rank, columns), 0)
    largest = jnp.maximum(within, row)
    masked = [[], []]
    for i in range(blocks):
        ranks = jnp.zeros((rank, columns), jnp.int32)
        for j in range(columns // rank):
            ranks = jnp.where(block_id == j, rank_ref[i, j], ranks)
        keep = largest < ranks
        for k in range(near_ref.shape[1]):
            keep = keep & (block_id != near_ref[i, k])
        for part in range(2):
            value = coupling_ref[i, part].astype(F32)
            masked[part].append(jnp.where(keep, value, 0.0).astype(BF16))
    masked = jnp.concatenate(masked[0] + masked[1], axis=0)
    both = jnp.dot(masked, gathered_ref[...], preferred_element_type=F32)
    mixed = (both[:size] + times_i_lanes(both[size:], inc)).astype(BF16).astype(F32)
    mixed = jnp.concatenate([mixed, times_i_lanes(mixed, inc)], axis=0).astype(BF16)
    row_block = lax.broadcasted_iota(jnp.int32, (size, block), 0) // rank
    basis = [
        jnp.concatenate([target_ref[i, part] for i in range(blocks)], axis=0).astype(F32)
        for part in range(2)
    ]
    half = block // 2
    high = lax.axis_index("inc") // (lax.axis_size("inc") // 2) == 1
    empty = jnp.zeros((2 * inc, half), F32)
    sent = lax.broadcasted_iota(jnp.int32, (block, 2 * block), 0)
    lane = lax.broadcasted_iota(jnp.int32, (block, 2 * block), 1)
    me_inc, groups = lax.axis_index("inc"), half // rows
    group = (sent // rows) % groups
    if bits > 1:
        group = lax.bitwise_xor(group, lax.bitwise_xor(me_inc, groups | 1))
    else:
        group = group + lax.bitwise_xor(me_inc // groups, 1) * groups
    target = (sent // half) * block + group * rows + sent % rows
    place_ref[...] = jnp.where(lane == target, 1.0, 0.0).astype(BF16)
    for pair in range(blocks // 2):
        own = keep_ref[:, pair * block : (pair + 1) * block]
        if bits > 1:
            own = in_order(own, bits, rows)
        for i in (2 * pair, 2 * pair + 1):
            spread = jnp.concatenate(
                [jnp.where(row_block == i, basis[part], 0.0) for part in range(2)], axis=0
            ).astype(BF16)
            far = tn_dot(mixed, spread)
            span = slice(i * block, (i + 1) * block)
            kept = own[:, (i - 2 * pair) * half : (i - 2 * pair + 1) * half]
            near = jnp.where(
                high, jnp.concatenate([empty, kept], axis=1), jnp.concatenate([kept, empty], axis=1)
            )
            field = jnp.concatenate([field_ref[0][:, span], field_ref[1][:, span]], axis=0)
            base_ref[:, span] = field.astype(F32) * 0.5 + near + far


def final_kernel(base_ref, got_ref, place_ref, out_ref):
    _, inc, panels = out_ref.shape
    block, width = place_ref.shape
    for pair in range(panels // width):
        near = jnp.dot(
            got_ref[:, pair * block : (pair + 1) * block],
            place_ref[...],
            preferred_element_type=F32,
        )
        span = slice(pair * width, (pair + 1) * width)
        result = (base_ref[:, span] + near).astype(BF16)
        out_ref[0, :, span] = result[:inc]
        out_ref[1, :, span] = result[inc:]


def call(kernel, name, out_shape, ins, out_specs, scratch=(), us=1.0, **more):
    return pl.pallas_call(
        kernel,
        out_shape=out_shape,
        in_specs=ins,
        out_specs=out_specs,
        scratch_shapes=list(scratch),
        compiler_params=params(),
        cost_estimate=cost(us),
        name=name,
        **more,
    )


def local(surface_field, near_block, near_index, source_basis, coupling, target_basis, far_rank):
    blocks, rows, slots, _, block = near_block.shape
    _, inc, panels = surface_field.shape
    rank = source_basis.shape[2]
    panel_count = lax.axis_size("panel")
    inc_count = lax.axis_size("inc")
    half = inc_count // 2
    swaps = panel_count == 4
    lines = rows * slots * 2

    def across(x, bit):
        return lax.ppermute(x, "inc", [(i, i ^ bit) for i in range(inc_count)])

    def onward(x, step, even=0, odd=0):
        if even:
            pairs = [
                (p * inc_count + i, (p ^ (odd if i % 2 else even)) * inc_count + i)
                for p in range(panel_count)
                for i in range(inc_count)
            ]
            return lax.ppermute(x, ("panel", "inc"), pairs)
        return lax.ppermute(
            x, "panel", [(i, (i - step) % panel_count) for i in range(panel_count)]
        )

    if swaps:
        order = [(0, 0, 0), (0, 1, 3), (0, 3, 1), (0, 2, 2)]
    else:
        order = [(0, 0, 0), (1, 0, 0), (panel_count - 1, 0, 0)]
        order += [(k, 0, 0) for k in range(2, panel_count - 1)]

    partner = half | 1
    other = across(surface_field, partner)
    raw = near_block.reshape(blocks * lines, block)
    paired = half == 4 and rows % 16 == 0
    if paired:
        token = call(
            token_kernel,
            "token",
            jax.ShapeDtypeStruct((8, 128), F32),
            [ANY],
            VMEM,
            us=0.1,
        )(in_hbm(surface_field))
        raw = call(
            stage_kernel,
            "stage",
            jax.ShapeDtypeStruct(raw.shape, BF16),
            [VMEM, ANY],
            VMEM,
            us=50.0,
        )(raw, token)
        beyond = across(raw, 2)
        mate = across(raw, 1)

    packed, field = call(
        compress_kernel,
        "compress",
        (
            jax.ShapeDtypeStruct((rank, blocks * 2 * inc), BF16),
            jax.ShapeDtypeStruct(surface_field.shape, BF16),
        ),
        [ANY] * 2,
        (VMEM, VMEM),
        [
            pltpu.VMEM(source_basis.shape, BF16),
            pltpu.SemaphoreType.DMA((2,)),
        ],
        us=0.2,
    )(in_hbm(surface_field), in_hbm(source_basis))
    payload, again = call(
        pack_kernel,
        "pack",
        (
            jax.ShapeDtypeStruct((blocks * 4 * inc + rank, block), BF16),
            jax.ShapeDtypeStruct(packed.shape, BF16),
        ),
        [VMEM] * 3,
        (VMEM, VMEM),
        us=100.0,
    )(field, other, packed)
    first = onward(payload, *order[1])
    second = onward(payload, *order[2])
    rest = [onward(again, *which) for which in order[3:]]

    sizes = (rows, slots, block, blocks, panel_count, swaps)
    width = blocks * half * rows
    near_shape = (
        jax.ShapeDtypeStruct((2 * inc, width), F32),
        jax.ShapeDtypeStruct((2 * inc, width), BF16),
    )
    wide = pltpu.VMEM((4 * inc, 3 * blocks * 2 * block), BF16)
    if paired:
        picked = (2 * blocks + 1) * 2 * rows
        shape = jax.ShapeDtypeStruct((blocks, picked, block), BF16)
        pick, own_turned, mate_turned = call(
            functools.partial(turn_first_kernel, sizes),
            "turn_first",
            (jax.ShapeDtypeStruct((blocks, picked, lines), BF16), shape, shape),
            [VMEM] * 3,
            (VMEM,) * 3,
            us=TURN,
        )(near_index, raw, mate)
        last = across(beyond, 1)
        beyond_turned = call(
            functools.partial(turn_one_kernel, blocks),
            "turn_beyond",
            shape,
            [VMEM] * 2,
            VMEM,
            us=TURN2,
        )(pick, beyond)
        wide = pltpu.VMEM((2 * inc, 3 * blocks * 2 * block), BF16)
        windows = (second, payload, first)
        turned = (own_turned, mate_turned, beyond_turned)
        part, filled = call(
            functools.partial(near_early_kernel, sizes, inc),
            "near_early",
            (near_shape[0], jax.ShapeDtypeStruct(wide.shape, BF16)),
            [VMEM] * 6,
            (VMEM, VMEM),
            us=EARLY,
        )(*windows, *turned)
        send, last_turned = call(
            functools.partial(near_last_kernel, sizes),
            "near_last",
            (near_shape[1], shape),
            [VMEM] * 4,
            (VMEM, VMEM),
        )(pick, last, filled, part)
        keep = call(
            functools.partial(near_keep_kernel, sizes, inc),
            "near_keep",
            near_shape[0],
            [VMEM] * 7,
            VMEM,
            [wide],
        )(*windows, *turned, last_turned)
    else:
        coefs = {0: near_block.reshape(blocks, rows, slots * 2 * block)}
        bit = half // 2
        while bit:
            for at in sorted(coefs):
                coefs[at | bit] = across(coefs[at], bit)
            bit //= 2
        me = lax.axis_index("inc") % half
        stacked = jnp.stack([coefs[at] for at in range(half)], axis=1)
        stacked = jnp.take(stacked, jnp.arange(half) ^ me, axis=1)
        stacked = stacked.reshape(blocks, half * rows, slots * 2 * block)
        keep, send = call(
            functools.partial(near_rows_kernel, sizes, inc),
            "near_rows",
            near_shape,
            [SMEM] + [VMEM] * 4,
            (VMEM, VMEM),
            [wide],
        )(near_index, stacked, second, payload, first)
    bits = half if paired else 1
    got = across(send, partner)

    base, place = call(
        functools.partial(base_kernel, order, inc, bits, rows),
        "base",
        (
            jax.ShapeDtypeStruct((2 * inc, panels), F32),
            jax.ShapeDtypeStruct((block, 2 * block), BF16),
        ),
        [SMEM] * 2 + [VMEM] * (4 + panel_count),
        (VMEM, VMEM),
        [pltpu.VMEM((panel_count * blocks * rank, 2 * inc), BF16)],
    )(near_index, far_rank, field, keep, coupling, target_basis, packed, first, second, *rest)

    return call(
        final_kernel,
        "final",
        jax.ShapeDtypeStruct((2, inc, panels), BF16),
        [VMEM] * 3,
        VMEM,
    )(base, got, place)


def solution(mesh):
    return jax.shard_map(
        local,
        mesh=mesh,
        in_specs=(
            P(None, "inc", "panel"),
            P("panel", "inc", None, None, None),
            P("panel", None),
            P("panel", None, None, None),
            P("panel", None, None, None),
            P("panel", None, None, None),
            P("panel", None),
        ),
        out_specs=P(None, "inc", "panel"),
        check_vma=False,
    )
```

```python
import functools

import jax
import jax.numpy as jnp
from jax import lax
from jax.experimental import pallas as pl
from jax.experimental.pallas import tpu as pltpu
from jax.sharding import PartitionSpec as P

F32 = jnp.float32
BF16 = jnp.bfloat16
VMEM = pl.BlockSpec(memory_space=pltpu.VMEM)
SMEM = pl.BlockSpec(memory_space=pltpu.SMEM)
ANY = pl.BlockSpec(memory_space=pl.ANY)


TURN = 3.0
TURN2 = 3.0
EARLY = 1.0


def params():
    return pltpu.CompilerParams(vmem_limit_bytes=8 * 1024 * 1024)


def cost(us):
    return pl.CostEstimate(flops=int(us * 1e9), bytes_accessed=0, transcendentals=0)


def in_hbm(x):
    return pltpu.with_memory_space_constraint(x, pltpu.HBM)


def token_kernel(in_ref, out_ref):
    out_ref[...] = jnp.zeros(out_ref.shape, F32)


def stage_kernel(in_ref, token_ref, out_ref):
    out_ref[...] = in_ref[...]


def nt_dot(left, right):
    return lax.dot_general(left, right, (((1,), (1,)), ((), ())), preferred_element_type=F32)


def tn_dot(left, right):
    return lax.dot_general(left, right, (((0,), (0,)), ((), ())), preferred_element_type=F32)


def times_i(pair_rows, width):
    return jnp.concatenate([-pair_rows[width:], pair_rows[:width]], axis=0)


def times_i_lanes(pair_lanes, width):
    return jnp.concatenate([-pair_lanes[:, width:], pair_lanes[:, :width]], axis=1)


def compress_kernel(field_hbm, basis_hbm, packed_ref, field_ref, basis_ref, sems):
    copies = [
        pltpu.make_async_copy(field_hbm, field_ref, sems.at[0]),
        pltpu.make_async_copy(basis_hbm, basis_ref, sems.at[1]),
    ]
    for copy in copies:
        copy.start()
    for copy in copies:
        copy.wait()
    _, inc, _ = field_ref.shape
    blocks, _, rank, block = basis_ref.shape
    pieces = []
    for j in range(blocks):
        basis = jnp.concatenate([basis_ref[j, 0], basis_ref[j, 1]], axis=0)
        field = jnp.concatenate(
            [field_ref[part][:, j * block : (j + 1) * block] for part in range(2)], axis=0
        )
        both = nt_dot(basis, field)
        pieces.append(both[:rank] + times_i_lanes(both[rank:], inc))
    packed_ref[...] = jnp.concatenate(pieces, axis=1).astype(BF16)


def pack_kernel(own_ref, other_ref, packed_ref, payload_ref, again_ref):
    _, inc, panels = own_ref.shape
    block = payload_ref.shape[1]
    for b in range(panels // block):
        for side, ref in enumerate((own_ref, other_ref)):
            for part in range(2):
                at = ((b * 2 + side) * 2 + part) * inc
                payload_ref[at : at + inc, :] = ref[part][:, b * block : (b + 1) * block]
    payload_ref[4 * inc * (panels // block) :, :] = packed_ref[...]
    again_ref[...] = packed_ref[...]


def fill_wide(wide_ref, window_refs, inc, blocks, block, sides):
    for w, refs in enumerate(window_refs):
        for b in range(blocks):
            at = (w * blocks + b) * 2 * block
            for n, side in enumerate(sides):
                start = (b * 2 + side) * 2 * inc
                piece = refs[0][start : start + 2 * inc, :]
                if len(refs) == 2:
                    odd = lax.rem(lax.axis_index("panel") + lax.axis_index("inc"), 2) == 1
                    piece = jnp.where(odd, refs[1][start : start + 2 * inc, :], piece)
                rows = slice(n * 2 * inc, (n + 1) * 2 * inc)
                wide_ref[rows, at : at + block] = piece
                wide_ref[rows, at + block : at + 2 * block] = times_i(piece, inc)


def pick_matrix(near_ref, i, rows, slots, blocks, panel_count):
    total = blocks * panel_count
    shape = ((2 * blocks + 1) * 2 * rows, rows * slots * 2)
    out = lax.broadcasted_iota(jnp.int32, shape, 0)
    col = lax.broadcasted_iota(jnp.int32, (1, shape[1]), 1)
    slot = (col // 2) % slots
    distance = jnp.zeros((1, shape[1]), jnp.int32)
    for k in range(slots):
        distance = jnp.where(slot == k, near_ref[i : i + 1, k : k + 1], distance)
    distance = distance - (lax.axis_index("panel") * blocks + i) + blocks
    distance = jnp.where(distance < 0, distance + total, distance)
    distance = jnp.where(distance >= total, distance - total, distance)
    source = (distance * 2 + col % 2) * rows + col // (2 * slots)
    return jnp.where(out == source, 1.0, 0.0).astype(BF16)


def turn(pick, piece_ref, i):
    lines = pick.shape[1]
    piece = piece_ref[i * lines : (i + 1) * lines, :]
    return jnp.dot(pick, piece, preferred_element_type=F32).astype(BF16)


def turn_first_kernel(sizes, near_ref, *refs):
    rows, slots, block, blocks, panel_count, swaps = sizes
    own_ref, mate_ref = refs[:2]
    pick_ref, own_out, mate_out = refs[-3:]
    for i in range(blocks):
        pick = pick_matrix(near_ref, i, rows, slots, blocks, panel_count)
        pick_ref[i] = pick
        own_out[i] = turn(pick, own_ref, i)
        mate_out[i] = turn(pick, mate_ref, i)


def turn_one_kernel(blocks, pick_ref, piece_ref, *refs):
    for i in range(blocks):
        refs[-1][i] = turn(pick_ref[i], piece_ref, i)


def near_early_kernel(sizes, inc, below_ref, own_ref, above_ref, *refs):
    block, blocks = sizes[2], sizes[3]
    part_ref, wide_ref = refs[-2:]
    fill_windows(sizes, inc, 1, (below_ref, own_ref, above_ref), wide_ref)
    pieces = [[ref.at[i] for ref in refs[:-2]] for i in range(blocks)]
    for pair in range(blocks // 2):
        total = pair_sum(sizes, pair, pieces, wide_ref)
        part_ref[:, pair * block : pair * block + total.shape[1]] = total


def near_last_kernel(sizes, pick_ref, last_ref, wide_ref, part_ref, send_ref, last_turned):
    rows, slots, block, blocks, panel_count, swaps = sizes
    values = [turn(pick_ref[i], last_ref, i) for i in range(blocks)]
    for i in range(blocks):
        last_turned[i] = values[i]
    for pair in range(blocks // 2):
        total = pair_sum(sizes, pair, [[value] for value in values], wide_ref)
        span = slice(pair * block, (pair + 1) * block - total.shape[1])
        both = jnp.concatenate([part_ref[:, span], total], axis=1)
        send_ref[:, pair * block : (pair + 1) * block] = both.astype(BF16)


def pair_sum(sizes, pair, pieces, wide_ref):
    rows, slots, block, blocks, panel_count, swaps = sizes
    reach = 2 * blocks
    total = None
    for j in range(2 * pair, 2 * pair + 2 + reach):
        coefs = []
        for i in (2 * pair, 2 * pair + 1):
            arrays = pieces[i]
            if not 0 <= j - i <= reach:
                coefs.append(jnp.zeros((len(arrays) * rows, 2 * block), BF16))
                continue
            at = (j - i) * 2 * rows
            coefs += [
                jnp.concatenate([x[at : at + rows, :], x[at + rows : at + 2 * rows, :]], axis=1)
                for x in arrays
            ]
        field = wide_ref[:, j * 2 * block : (j + 1) * 2 * block]
        term = nt_dot(field, jnp.concatenate(coefs, axis=0))
        total = term if total is None else total + term
    return total


def near_keep_kernel(sizes, inc, below_ref, own_ref, above_ref, *refs):
    block, blocks = sizes[2], sizes[3]
    keep_ref, wide_ref = refs[-2:]
    fill_windows(sizes, inc, 0, (below_ref, own_ref, above_ref), wide_ref)
    sums = near_sums(sizes, refs[:-2], wide_ref)
    for pair in range(blocks // 2):
        span = slice(pair * block, (pair + 1) * block)
        keep_ref[:, span] = jnp.concatenate(sums[2 * pair : 2 * pair + 2], axis=1)


def fill_windows(sizes, inc, side, windows, wide_ref):
    rows, slots, block, blocks, panel_count, swaps = sizes
    below_ref, own_ref, above_ref = windows
    low, high = ((below_ref, above_ref), (above_ref, below_ref)) if swaps else ((below_ref,), (above_ref,))
    fill_wide(wide_ref, (low, (own_ref,), high), inc, blocks, block, (side,))


def near_sums(sizes, turned, wide_ref):
    rows, slots, block, blocks, panel_count, swaps = sizes
    sums = []
    for i in range(blocks):
        total = None
        for step in range(2 * blocks + 1):
            at = step * 2 * rows
            coefs = [
                jnp.concatenate(
                    [ref[i, at : at + rows, :], ref[i, at + rows : at + 2 * rows, :]], axis=1
                )
                for ref in turned
            ]
            coefs = coefs[0] if len(coefs) == 1 else jnp.concatenate(coefs, axis=0)
            start = (i + step) * 2 * block
            term = nt_dot(wide_ref[:, start : start + 2 * block], coefs)
            total = term if total is None else total + term
        sums.append(total)
    return sums


def near_rows_kernel(sizes, inc, near_ref, coefs_ref, below_ref, own_ref, above_ref, *refs):
    rows, slots, block, blocks, panel_count, swaps = sizes
    keep_ref, send_ref, wide_ref = refs
    low, high = ((below_ref, above_ref), (above_ref, below_ref)) if swaps else ((below_ref,), (above_ref,))
    fill_wide(wide_ref, (low, (own_ref,), high), inc, blocks, block, (0, 1))
    total_blocks = blocks * panel_count
    me = lax.axis_index("panel")
    half = coefs_ref.shape[1]
    for i in range(blocks):
        total = None
        for k in range(slots):
            at = near_ref[i, k] - (me * blocks + i) + blocks
            at = jnp.where(at < 0, at + total_blocks, at)
            at = jnp.where(at >= total_blocks, at - total_blocks, at)
            start = pl.multiple_of(jnp.minimum(at + i, 3 * blocks - 1) * (2 * block), 2 * block)
            coefs = coefs_ref[i, :, k * 2 * block : (k + 1) * 2 * block]
            term = nt_dot(wide_ref[:, pl.ds(start, 2 * block)], coefs)
            total = term if total is None else total + term
        span = slice(i * half, (i + 1) * half)
        keep_ref[:, span] = total[: 2 * inc]
        send_ref[:, span] = total[2 * inc :].astype(BF16)


def in_order(rows_of, bits, rows):
    lanes = rows_of.shape[1]
    lane = lax.broadcasted_iota(jnp.int32, rows_of.shape, 1)
    me = lax.axis_index("inc")
    bit = 1
    while bit < bits:
        shift = bit * rows
        upper = (lane // shift) % 2 == 1
        swapped = jnp.where(
            upper, pltpu.roll(rows_of, shift, 1), pltpu.roll(rows_of, lanes - shift, 1)
        )
        rows_of = jnp.where((me // bit) % 2 == 1, swapped, rows_of)
        bit *= 2
    return rows_of


def base_kernel(
    order, inc, bits, rows, near_ref, rank_ref, field_ref, keep_ref, coupling_ref, target_ref, *refs
):
    count = len(order)
    piece_refs = refs[:count]
    base_ref, place_ref, gathered_ref = refs[count:]
    blocks, _, rank, columns = coupling_ref.shape
    block = target_ref.shape[3]
    size = blocks * rank
    me = lax.axis_index("panel")
    core = lax.rem(lax.axis_index("inc"), 2)
    for ref, (step, even, odd) in zip(piece_refs, order):
        swap = jnp.where(core == 1, odd, even)
        at = lax.bitwise_xor(me, swap) if even else lax.rem(me + step, count)
        piece = ref[ref.shape[0] - rank :, :]
        for j in range(blocks):
            row = pl.multiple_of(at * size + j * rank, rank)
            gathered_ref[pl.ds(row, rank), :] = piece[:, j * 2 * inc : (j + 1) * 2 * inc]
    block_id = lax.broadcasted_iota(jnp.int32, (rank, columns), 1) // rank
    within = lax.broadcasted_iota(jnp.int32, (rank, columns), 1) % rank
    row = lax.broadcasted_iota(jnp.int32, (rank, columns), 0)
    largest = jnp.maximum(within, row)
    masked = [[], []]
    for i in range(blocks):
        ranks = jnp.zeros((rank, columns), jnp.int32)
        for j in range(columns // rank):
            ranks = jnp.where(block_id == j, rank_ref[i, j], ranks)
        keep = largest < ranks
        for k in range(near_ref.shape[1]):
            keep = keep & (block_id != near_ref[i, k])
        for part in range(2):
            value = coupling_ref[i, part].astype(F32)
            masked[part].append(jnp.where(keep, value, 0.0).astype(BF16))
    masked = jnp.concatenate(masked[0] + masked[1], axis=0)
    both = jnp.dot(masked, gathered_ref[...], preferred_element_type=F32)
    mixed = (both[:size] + times_i_lanes(both[size:], inc)).astype(BF16).astype(F32)
    mixed = jnp.concatenate([mixed, times_i_lanes(mixed, inc)], axis=0).astype(BF16)
    row_block = lax.broadcasted_iota(jnp.int32, (size, block), 0) // rank
    basis = [
        jnp.concatenate([target_ref[i, part] for i in range(blocks)], axis=0).astype(F32)
        for part in range(2)
    ]
    half = block // 2
    high = lax.axis_index("inc") // (lax.axis_size("inc") // 2) == 1
    empty = jnp.zeros((2 * inc, half), F32)
    sent = lax.broadcasted_iota(jnp.int32, (block, 2 * block), 0)
    lane = lax.broadcasted_iota(jnp.int32, (block, 2 * block), 1)
    me_inc, groups = lax.axis_index("inc"), half // rows
    group = (sent // rows) % groups
    which = sent // half
    if bits > 1:
        early = 2 * half - 2 * rows
        group = jnp.where(sent < early, (sent // rows) % (groups - 1), groups - 1)
        which = jnp.where(sent < early, sent // (half - rows), (sent - early) // rows)
        group = lax.bitwise_xor(group, lax.bitwise_xor(me_inc, groups | 1))
    else:
        group = group + lax.bitwise_xor(me_inc // groups, 1) * groups
    target = which * block + group * rows + sent % rows
    place_ref[...] = jnp.where(lane == target, 1.0, 0.0).astype(BF16)
    for pair in range(blocks // 2):
        own = keep_ref[:, pair * block : (pair + 1) * block]
        if bits > 1:
            own = in_order(own, bits, rows)
        for i in (2 * pair, 2 * pair + 1):
            spread = jnp.concatenate(
                [jnp.where(row_block == i, basis[part], 0.0) for part in range(2)], axis=0
            ).astype(BF16)
            far = tn_dot(mixed, spread)
            span = slice(i * block, (i + 1) * block)
            kept = own[:, (i - 2 * pair) * half : (i - 2 * pair + 1) * half]
            near = jnp.where(
                high, jnp.concatenate([empty, kept], axis=1), jnp.concatenate([kept, empty], axis=1)
            )
            field = jnp.concatenate([field_ref[0][:, span], field_ref[1][:, span]], axis=0)
            base_ref[:, span] = field.astype(F32) * 0.5 + near + far


def final_kernel(base_ref, got_ref, place_ref, out_ref):
    _, inc, panels = out_ref.shape
    block, width = place_ref.shape
    for pair in range(panels // width):
        near = jnp.dot(
            got_ref[:, pair * block : (pair + 1) * block],
            place_ref[...],
            preferred_element_type=F32,
        )
        span = slice(pair * width, (pair + 1) * width)
        result = (base_ref[:, span] + near).astype(BF16)
        out_ref[0, :, span] = result[:inc]
        out_ref[1, :, span] = result[inc:]


def call(kernel, name, out_shape, ins, out_specs, scratch=(), us=1.0, **more):
    return pl.pallas_call(
        kernel,
        out_shape=out_shape,
        in_specs=ins,
        out_specs=out_specs,
        scratch_shapes=list(scratch),
        compiler_params=params(),
        cost_estimate=cost(us),
        name=name,
        **more,
    )


def local(surface_field, near_block, near_index, source_basis, coupling, target_basis, far_rank):
    blocks, rows, slots, _, block = near_block.shape
    _, inc, panels = surface_field.shape
    rank = source_basis.shape[2]
    panel_count = lax.axis_size("panel")
    inc_count = lax.axis_size("inc")
    half = inc_count // 2
    swaps = panel_count == 4
    lines = rows * slots * 2

    def across(x, bit):
        return lax.ppermute(x, "inc", [(i, i ^ bit) for i in range(inc_count)])

    def onward(x, step, even=0, odd=0):
        if even:
            pairs = [
                (p * inc_count + i, (p ^ (odd if i % 2 else even)) * inc_count + i)
                for p in range(panel_count)
                for i in range(inc_count)
            ]
            return lax.ppermute(x, ("panel", "inc"), pairs)
        return lax.ppermute(
            x, "panel", [(i, (i - step) % panel_count) for i in range(panel_count)]
        )

    if swaps:
        order = [(0, 0, 0), (0, 1, 3), (0, 3, 1), (0, 2, 2)]
    else:
        order = [(0, 0, 0), (1, 0, 0), (panel_count - 1, 0, 0)]
        order += [(k, 0, 0) for k in range(2, panel_count - 1)]

    partner = half | 1
    other = across(surface_field, partner)
    raw = near_block.reshape(blocks * lines, block)
    paired = half == 4 and rows % 16 == 0
    if paired:
        token = call(
            token_kernel,
            "token",
            jax.ShapeDtypeStruct((8, 128), F32),
            [ANY],
            VMEM,
            us=0.1,
        )(in_hbm(surface_field))
        raw = call(
            stage_kernel,
            "stage",
            jax.ShapeDtypeStruct(raw.shape, BF16),
            [VMEM, ANY],
            VMEM,
            us=50.0,
        )(raw, token)
        beyond = across(raw, 2)
        mate = across(raw, 1)

    packed, field = call(
        compress_kernel,
        "compress",
        (
            jax.ShapeDtypeStruct((rank, blocks * 2 * inc), BF16),
            jax.ShapeDtypeStruct(surface_field.shape, BF16),
        ),
        [ANY] * 2,
        (VMEM, VMEM),
        [
            pltpu.VMEM(source_basis.shape, BF16),
            pltpu.SemaphoreType.DMA((2,)),
        ],
        us=0.2,
    )(in_hbm(surface_field), in_hbm(source_basis))
    payload, again = call(
        pack_kernel,
        "pack",
        (
            jax.ShapeDtypeStruct((blocks * 4 * inc + rank, block), BF16),
            jax.ShapeDtypeStruct(packed.shape, BF16),
        ),
        [VMEM] * 3,
        (VMEM, VMEM),
        us=100.0,
    )(field, other, packed)
    first = onward(payload, *order[1])
    second = onward(payload, *order[2])
    rest = [onward(again, *which) for which in order[3:]]

    sizes = (rows, slots, block, blocks, panel_count, swaps)
    width = blocks * half * rows
    near_shape = (
        jax.ShapeDtypeStruct((2 * inc, width), F32),
        jax.ShapeDtypeStruct((2 * inc, width), BF16),
    )
    wide = pltpu.VMEM((4 * inc, 3 * blocks * 2 * block), BF16)
    if paired:
        picked = (2 * blocks + 1) * 2 * rows
        shape = jax.ShapeDtypeStruct((blocks, picked, block), BF16)
        pick, own_turned, mate_turned = call(
            functools.partial(turn_first_kernel, sizes),
            "turn_first",
            (jax.ShapeDtypeStruct((blocks, picked, lines), BF16), shape, shape),
            [VMEM] * 3,
            (VMEM,) * 3,
            us=TURN,
        )(near_index, raw, mate)
        last = across(beyond, 1)
        beyond_turned = call(
            functools.partial(turn_one_kernel, blocks),
            "turn_beyond",
            shape,
            [VMEM] * 2,
            VMEM,
            us=TURN2,
        )(pick, beyond)
        wide = pltpu.VMEM((2 * inc, 3 * blocks * 2 * block), BF16)
        windows = (second, payload, first)
        turned = (own_turned, mate_turned, beyond_turned)
        part, filled = call(
            functools.partial(near_early_kernel, sizes, inc),
            "near_early",
            (near_shape[0], jax.ShapeDtypeStruct(wide.shape, BF16)),
            [VMEM] * 6,
            (VMEM, VMEM),
            us=EARLY,
        )(*windows, *turned)
        send, last_turned = call(
            functools.partial(near_last_kernel, sizes),
            "near_last",
            (near_shape[1], shape),
            [VMEM] * 4,
            (VMEM, VMEM),
        )(pick, last, filled, part)
        keep = call(
            functools.partial(near_keep_kernel, sizes, inc),
            "near_keep",
            near_shape[0],
            [VMEM] * 7,
            VMEM,
            [wide],
        )(*windows, *turned, last_turned)
    else:
        coefs = {0: near_block.reshape(blocks, rows, slots * 2 * block)}
        bit = half // 2
        while bit:
            for at in sorted(coefs):
                coefs[at | bit] = across(coefs[at], bit)
            bit //= 2
        me = lax.axis_index("inc") % half
        stacked = jnp.stack([coefs[at] for at in range(half)], axis=1)
        stacked = jnp.take(stacked, jnp.arange(half) ^ me, axis=1)
        stacked = stacked.reshape(blocks, half * rows, slots * 2 * block)
        keep, send = call(
            functools.partial(near_rows_kernel, sizes, inc),
            "near_rows",
            near_shape,
            [SMEM] + [VMEM] * 4,
            (VMEM, VMEM),
            [wide],
        )(near_index, stacked, second, payload, first)
    bits = half if paired else 1
    got = across(send, partner)

    base, place = call(
        functools.partial(base_kernel, order, inc, bits, rows),
        "base",
        (
            jax.ShapeDtypeStruct((2 * inc, panels), F32),
            jax.ShapeDtypeStruct((block, 2 * block), BF16),
        ),
        [SMEM] * 2 + [VMEM] * (4 + panel_count),
        (VMEM, VMEM),
        [pltpu.VMEM((panel_count * blocks * rank, 2 * inc), BF16)],
    )(near_index, far_rank, field, keep, coupling, target_basis, packed, first, second, *rest)

    return call(
        final_kernel,
        "final",
        jax.ShapeDtypeStruct((2, inc, panels), BF16),
        [VMEM] * 3,
        VMEM,
    )(base, got, place)


def solution(mesh):
    return jax.shard_map(
        local,
        mesh=mesh,
        in_specs=(
            P(None, "inc", "panel"),
            P("panel", "inc", None, None, None),
            P("panel", None),
            P("panel", None, None, None),
            P("panel", None, None, None),
            P("panel", None, None, None),
            P("panel", None),
        ),
        out_specs=P(None, "inc", "panel"),
        check_vma=False,
    )
```

```python
import functools

import jax
import jax.numpy as jnp
from jax import lax
from jax.experimental import pallas as pl
from jax.experimental.pallas import tpu as pltpu
from jax.sharding import PartitionSpec as P

F32 = jnp.float32
BF16 = jnp.bfloat16
VMEM = pl.BlockSpec(memory_space=pltpu.VMEM)
SMEM = pl.BlockSpec(memory_space=pltpu.SMEM)
ANY = pl.BlockSpec(memory_space=pl.ANY)


TURN = 3.0
TURN2 = 3.0
EARLY = 1.0


def params():
    return pltpu.CompilerParams(vmem_limit_bytes=8 * 1024 * 1024)


def cost(us):
    return pl.CostEstimate(flops=int(us * 1e9), bytes_accessed=0, transcendentals=0)


def in_hbm(x):
    return pltpu.with_memory_space_constraint(x, pltpu.HBM)


def token_kernel(in_ref, out_ref):
    out_ref[...] = jnp.zeros(out_ref.shape, F32)


def stage_kernel(in_ref, token_ref, out_ref):
    out_ref[...] = in_ref[...]


def nt_dot(left, right):
    return lax.dot_general(left, right, (((1,), (1,)), ((), ())), preferred_element_type=F32)


def tn_dot(left, right):
    return lax.dot_general(left, right, (((0,), (0,)), ((), ())), preferred_element_type=F32)


def times_i(pair_rows, width):
    return jnp.concatenate([-pair_rows[width:], pair_rows[:width]], axis=0)


def times_i_lanes(pair_lanes, width):
    return jnp.concatenate([-pair_lanes[:, width:], pair_lanes[:, :width]], axis=1)


def compress_kernel(own_ref, basis_ref, packed_ref, field_ref):
    field_ref[...] = own_ref[...]
    _, inc, _ = field_ref.shape
    blocks, _, rank, block = basis_ref.shape
    pieces = []
    for j in range(blocks):
        basis = jnp.concatenate([basis_ref[j, 0], basis_ref[j, 1]], axis=0)
        field = jnp.concatenate(
            [field_ref[part][:, j * block : (j + 1) * block] for part in range(2)], axis=0
        )
        both = nt_dot(basis, field)
        pieces.append(both[:rank] + times_i_lanes(both[rank:], inc))
    packed_ref[...] = jnp.concatenate(pieces, axis=1).astype(BF16)


def pack_kernel(own_ref, other_ref, packed_ref, payload_ref, again_ref):
    _, inc, panels = own_ref.shape
    block = payload_ref.shape[1]
    for b in range(panels // block):
        for side, ref in enumerate((own_ref, other_ref)):
            for part in range(2):
                at = ((b * 2 + side) * 2 + part) * inc
                payload_ref[at : at + inc, :] = ref[part][:, b * block : (b + 1) * block]
    payload_ref[4 * inc * (panels // block) :, :] = packed_ref[...]
    again_ref[...] = packed_ref[...]


def fill_wide(wide_ref, window_refs, inc, blocks, block, sides):
    for w, refs in enumerate(window_refs):
        for b in range(blocks):
            at = (w * blocks + b) * 2 * block
            for n, side in enumerate(sides):
                start = (b * 2 + side) * 2 * inc
                piece = refs[0][start : start + 2 * inc, :]
                if len(refs) == 2:
                    odd = lax.rem(lax.axis_index("panel") + lax.axis_index("inc"), 2) == 1
                    piece = jnp.where(odd, refs[1][start : start + 2 * inc, :], piece)
                rows = slice(n * 2 * inc, (n + 1) * 2 * inc)
                wide_ref[rows, at : at + block] = piece
                wide_ref[rows, at + block : at + 2 * block] = times_i(piece, inc)


def pick_matrix(near_ref, i, rows, slots, blocks, panel_count):
    total = blocks * panel_count
    shape = ((2 * blocks + 1) * 2 * rows, rows * slots * 2)
    out = lax.broadcasted_iota(jnp.int32, shape, 0)
    col = lax.broadcasted_iota(jnp.int32, (1, shape[1]), 1)
    slot = (col // 2) % slots
    distance = jnp.zeros((1, shape[1]), jnp.int32)
    for k in range(slots):
        distance = jnp.where(slot == k, near_ref[i : i + 1, k : k + 1], distance)
    distance = distance - (lax.axis_index("panel") * blocks + i) + blocks
    distance = jnp.where(distance < 0, distance + total, distance)
    distance = jnp.where(distance >= total, distance - total, distance)
    source = (distance * 2 + col % 2) * rows + col // (2 * slots)
    return jnp.where(out == source, 1.0, 0.0).astype(BF16)


def turn(pick, piece_ref, i):
    lines = pick.shape[1]
    piece = piece_ref[i * lines : (i + 1) * lines, :]
    return jnp.dot(pick, piece, preferred_element_type=F32).astype(BF16)


def turn_first_kernel(sizes, near_ref, *refs):
    rows, slots, block, blocks, panel_count, swaps = sizes
    own_ref, mate_ref = refs[:2]
    pick_ref, own_out, mate_out = refs[-3:]
    for i in range(blocks):
        pick = pick_matrix(near_ref, i, rows, slots, blocks, panel_count)
        pick_ref[i] = pick
        own_out[i] = turn(pick, own_ref, i)
        mate_out[i] = turn(pick, mate_ref, i)


def turn_one_kernel(blocks, pick_ref, piece_ref, *refs):
    for i in range(blocks):
        refs[-1][i] = turn(pick_ref[i], piece_ref, i)


def near_early_kernel(sizes, inc, below_ref, own_ref, above_ref, *refs):
    block, blocks = sizes[2], sizes[3]
    part_ref, wide_ref = refs[-2:]
    fill_windows(sizes, inc, 1, (below_ref, own_ref, above_ref), wide_ref)
    pieces = [[ref.at[i] for ref in refs[:-2]] for i in range(blocks)]
    for pair in range(blocks // 2):
        total = pair_sum(sizes, pair, pieces, wide_ref)
        part_ref[:, pair * block : pair * block + total.shape[1]] = total


def near_last_kernel(sizes, pick_ref, last_ref, wide_ref, part_ref, send_ref, last_turned):
    rows, slots, block, blocks, panel_count, swaps = sizes
    values = [turn(pick_ref[i], last_ref, i) for i in range(blocks)]
    for i in range(blocks):
        last_turned[i] = values[i]
    for pair in range(blocks // 2):
        total = pair_sum(sizes, pair, [[value] for value in values], wide_ref)
        span = slice(pair * block, (pair + 1) * block - total.shape[1])
        both = jnp.concatenate([part_ref[:, span], total], axis=1)
        send_ref[:, pair * block : (pair + 1) * block] = both.astype(BF16)


def pair_sum(sizes, pair, pieces, wide_ref):
    rows, slots, block, blocks, panel_count, swaps = sizes
    reach = 2 * blocks
    total = None
    for j in range(2 * pair, 2 * pair + 2 + reach):
        coefs = []
        for i in (2 * pair, 2 * pair + 1):
            arrays = pieces[i]
            if not 0 <= j - i <= reach:
                coefs.append(jnp.zeros((len(arrays) * rows, 2 * block), BF16))
                continue
            at = (j - i) * 2 * rows
            coefs += [
                jnp.concatenate([x[at : at + rows, :], x[at + rows : at + 2 * rows, :]], axis=1)
                for x in arrays
            ]
        field = wide_ref[:, j * 2 * block : (j + 1) * 2 * block]
        term = nt_dot(field, jnp.concatenate(coefs, axis=0))
        total = term if total is None else total + term
    return total


def near_keep_kernel(sizes, inc, below_ref, own_ref, above_ref, *refs):
    block, blocks = sizes[2], sizes[3]
    keep_ref, wide_ref = refs[-2:]
    fill_windows(sizes, inc, 0, (below_ref, own_ref, above_ref), wide_ref)
    sums = near_sums(sizes, refs[:-2], wide_ref)
    for pair in range(blocks // 2):
        span = slice(pair * block, (pair + 1) * block)
        keep_ref[:, span] = jnp.concatenate(sums[2 * pair : 2 * pair + 2], axis=1)


def fill_windows(sizes, inc, side, windows, wide_ref):
    rows, slots, block, blocks, panel_count, swaps = sizes
    below_ref, own_ref, above_ref = windows
    low, high = ((below_ref, above_ref), (above_ref, below_ref)) if swaps else ((below_ref,), (above_ref,))
    fill_wide(wide_ref, (low, (own_ref,), high), inc, blocks, block, (side,))


def near_sums(sizes, turned, wide_ref):
    rows, slots, block, blocks, panel_count, swaps = sizes
    sums = []
    for i in range(blocks):
        total = None
        for step in range(2 * blocks + 1):
            at = step * 2 * rows
            coefs = [
                jnp.concatenate(
                    [ref[i, at : at + rows, :], ref[i, at + rows : at + 2 * rows, :]], axis=1
                )
                for ref in turned
            ]
            coefs = coefs[0] if len(coefs) == 1 else jnp.concatenate(coefs, axis=0)
            start = (i + step) * 2 * block
            term = nt_dot(wide_ref[:, start : start + 2 * block], coefs)
            total = term if total is None else total + term
        sums.append(total)
    return sums


def near_rows_kernel(sizes, inc, near_ref, coefs_ref, below_ref, own_ref, above_ref, *refs):
    rows, slots, block, blocks, panel_count, swaps = sizes
    keep_ref, send_ref, wide_ref = refs
    low, high = ((below_ref, above_ref), (above_ref, below_ref)) if swaps else ((below_ref,), (above_ref,))
    fill_wide(wide_ref, (low, (own_ref,), high), inc, blocks, block, (0, 1))
    total_blocks = blocks * panel_count
    me = lax.axis_index("panel")
    half = coefs_ref.shape[1]
    for i in range(blocks):
        total = None
        for k in range(slots):
            at = near_ref[i, k] - (me * blocks + i) + blocks
            at = jnp.where(at < 0, at + total_blocks, at)
            at = jnp.where(at >= total_blocks, at - total_blocks, at)
            start = pl.multiple_of(jnp.minimum(at + i, 3 * blocks - 1) * (2 * block), 2 * block)
            coefs = coefs_ref[i, :, k * 2 * block : (k + 1) * 2 * block]
            term = nt_dot(wide_ref[:, pl.ds(start, 2 * block)], coefs)
            total = term if total is None else total + term
        span = slice(i * half, (i + 1) * half)
        keep_ref[:, span] = total[: 2 * inc]
        send_ref[:, span] = total[2 * inc :].astype(BF16)


def in_order(rows_of, bits, rows):
    lanes = rows_of.shape[1]
    lane = lax.broadcasted_iota(jnp.int32, rows_of.shape, 1)
    me = lax.axis_index("inc")
    bit = 1
    while bit < bits:
        shift = bit * rows
        upper = (lane // shift) % 2 == 1
        swapped = jnp.where(
            upper, pltpu.roll(rows_of, shift, 1), pltpu.roll(rows_of, lanes - shift, 1)
        )
        rows_of = jnp.where((me // bit) % 2 == 1, swapped, rows_of)
        bit *= 2
    return rows_of


def base_kernel(
    order, inc, bits, rows, near_ref, rank_ref, field_ref, keep_ref, coupling_ref, target_ref, *refs
):
    count = len(order)
    piece_refs = refs[:count]
    base_ref, place_ref, gathered_ref = refs[count:]
    blocks, _, rank, columns = coupling_ref.shape
    block = target_ref.shape[3]
    size = blocks * rank
    me = lax.axis_index("panel")
    core = lax.rem(lax.axis_index("inc"), 2)
    for ref, (step, even, odd) in zip(piece_refs, order):
        swap = jnp.where(core == 1, odd, even)
        at = lax.bitwise_xor(me, swap) if even else lax.rem(me + step, count)
        piece = ref[ref.shape[0] - rank :, :]
        for j in range(blocks):
            row = pl.multiple_of(at * size + j * rank, rank)
            gathered_ref[pl.ds(row, rank), :] = piece[:, j * 2 * inc : (j + 1) * 2 * inc]
    block_id = lax.broadcasted_iota(jnp.int32, (rank, columns), 1) // rank
    within = lax.broadcasted_iota(jnp.int32, (rank, columns), 1) % rank
    row = lax.broadcasted_iota(jnp.int32, (rank, columns), 0)
    largest = jnp.maximum(within, row)
    masked = [[], []]
    for i in range(blocks):
        ranks = jnp.zeros((rank, columns), jnp.int32)
        for j in range(columns // rank):
            ranks = jnp.where(block_id == j, rank_ref[i, j], ranks)
        keep = largest < ranks
        for k in range(near_ref.shape[1]):
            keep = keep & (block_id != near_ref[i, k])
        for part in range(2):
            value = coupling_ref[i, part].astype(F32)
            masked[part].append(jnp.where(keep, value, 0.0).astype(BF16))
    masked = jnp.concatenate(masked[0] + masked[1], axis=0)
    both = jnp.dot(masked, gathered_ref[...], preferred_element_type=F32)
    mixed = (both[:size] + times_i_lanes(both[size:], inc)).astype(BF16).astype(F32)
    mixed = jnp.concatenate([mixed, times_i_lanes(mixed, inc)], axis=0).astype(BF16)
    row_block = lax.broadcasted_iota(jnp.int32, (size, block), 0) // rank
    basis = [
        jnp.concatenate([target_ref[i, part] for i in range(blocks)], axis=0).astype(F32)
        for part in range(2)
    ]
    half = block // 2
    high = lax.axis_index("inc") // (lax.axis_size("inc") // 2) == 1
    empty = jnp.zeros((2 * inc, half), F32)
    sent = lax.broadcasted_iota(jnp.int32, (block, 2 * block), 0)
    lane = lax.broadcasted_iota(jnp.int32, (block, 2 * block), 1)
    me_inc, groups = lax.axis_index("inc"), half // rows
    group = (sent // rows) % groups
    which = sent // half
    if bits > 1:
        early = 2 * half - 2 * rows
        group = jnp.where(sent < early, (sent // rows) % (groups - 1), groups - 1)
        which = jnp.where(sent < early, sent // (half - rows), (sent - early) // rows)
        group = lax.bitwise_xor(group, lax.bitwise_xor(me_inc, groups | 1))
    else:
        group = group + lax.bitwise_xor(me_inc // groups, 1) * groups
    target = which * block + group * rows + sent % rows
    place_ref[...] = jnp.where(lane == target, 1.0, 0.0).astype(BF16)
    for pair in range(blocks // 2):
        own = keep_ref[:, pair * block : (pair + 1) * block]
        if bits > 1:
            own = in_order(own, bits, rows)
        for i in (2 * pair, 2 * pair + 1):
            spread = jnp.concatenate(
                [jnp.where(row_block == i, basis[part], 0.0) for part in range(2)], axis=0
            ).astype(BF16)
            far = tn_dot(mixed, spread)
            span = slice(i * block, (i + 1) * block)
            kept = own[:, (i - 2 * pair) * half : (i - 2 * pair + 1) * half]
            near = jnp.where(
                high, jnp.concatenate([empty, kept], axis=1), jnp.concatenate([kept, empty], axis=1)
            )
            field = jnp.concatenate([field_ref[0][:, span], field_ref[1][:, span]], axis=0)
            base_ref[:, span] = field.astype(F32) * 0.5 + near + far


def final_kernel(base_ref, got_ref, place_ref, out_ref):
    _, inc, panels = out_ref.shape
    block, width = place_ref.shape
    for pair in range(panels // width):
        near = jnp.dot(
            got_ref[:, pair * block : (pair + 1) * block],
            place_ref[...],
            preferred_element_type=F32,
        )
        span = slice(pair * width, (pair + 1) * width)
        result = (base_ref[:, span] + near).astype(BF16)
        out_ref[0, :, span] = result[:inc]
        out_ref[1, :, span] = result[inc:]


def call(kernel, name, out_shape, ins, out_specs, scratch=(), us=1.0, **more):
    return pl.pallas_call(
        kernel,
        out_shape=out_shape,
        in_specs=ins,
        out_specs=out_specs,
        scratch_shapes=list(scratch),
        compiler_params=params(),
        cost_estimate=cost(us),
        name=name,
        **more,
    )


def local(surface_field, near_block, near_index, source_basis, coupling, target_basis, far_rank):
    blocks, rows, slots, _, block = near_block.shape
    _, inc, panels = surface_field.shape
    rank = source_basis.shape[2]
    panel_count = lax.axis_size("panel")
    inc_count = lax.axis_size("inc")
    half = inc_count // 2
    swaps = panel_count == 4
    lines = rows * slots * 2

    def across(x, bit):
        return lax.ppermute(x, "inc", [(i, i ^ bit) for i in range(inc_count)])

    def onward(x, step, even=0, odd=0):
        if even:
            pairs = [
                (p * inc_count + i, (p ^ (odd if i % 2 else even)) * inc_count + i)
                for p in range(panel_count)
                for i in range(inc_count)
            ]
            return lax.ppermute(x, ("panel", "inc"), pairs)
        return lax.ppermute(
            x, "panel", [(i, (i - step) % panel_count) for i in range(panel_count)]
        )

    if swaps:
        order = [(0, 0, 0), (0, 1, 3), (0, 3, 1), (0, 2, 2)]
    else:
        order = [(0, 0, 0), (1, 0, 0), (panel_count - 1, 0, 0)]
        order += [(k, 0, 0) for k in range(2, panel_count - 1)]

    partner = half | 1
    other = across(surface_field, partner)
    raw = near_block.reshape(blocks * lines, block)
    paired = half == 4 and rows % 16 == 0
    if paired:
        token = call(
            token_kernel,
            "token",
            jax.ShapeDtypeStruct((8, 128), F32),
            [ANY],
            VMEM,
            us=0.1,
        )(in_hbm(surface_field))
        raw = call(
            stage_kernel,
            "stage",
            jax.ShapeDtypeStruct(raw.shape, BF16),
            [VMEM, ANY],
            VMEM,
            us=50.0,
        )(raw, token)
        beyond = across(raw, 2)
        mate = across(raw, 1)

    packed, field = call(
        compress_kernel,
        "compress",
        (
            jax.ShapeDtypeStruct((rank, blocks * 2 * inc), BF16),
            jax.ShapeDtypeStruct(surface_field.shape, BF16),
        ),
        [VMEM] * 2,
        (VMEM, VMEM),
        us=0.2,
    )(surface_field, source_basis)
    payload, again = call(
        pack_kernel,
        "pack",
        (
            jax.ShapeDtypeStruct((blocks * 4 * inc + rank, block), BF16),
            jax.ShapeDtypeStruct(packed.shape, BF16),
        ),
        [VMEM] * 3,
        (VMEM, VMEM),
        us=100.0,
    )(field, other, packed)
    first = onward(payload, *order[1])
    second = onward(payload, *order[2])
    rest = [onward(again, *which) for which in order[3:]]

    sizes = (rows, slots, block, blocks, panel_count, swaps)
    width = blocks * half * rows
    near_shape = (
        jax.ShapeDtypeStruct((2 * inc, width), F32),
        jax.ShapeDtypeStruct((2 * inc, width), BF16),
    )
    wide = pltpu.VMEM((4 * inc, 3 * blocks * 2 * block), BF16)
    if paired:
        picked = (2 * blocks + 1) * 2 * rows
        shape = jax.ShapeDtypeStruct((blocks, picked, block), BF16)
        pick, own_turned, mate_turned = call(
            functools.partial(turn_first_kernel, sizes),
            "turn_first",
            (jax.ShapeDtypeStruct((blocks, picked, lines), BF16), shape, shape),
            [VMEM] * 3,
            (VMEM,) * 3,
            us=TURN,
        )(near_index, raw, mate)
        last = across(beyond, 1)
        beyond_turned = call(
            functools.partial(turn_one_kernel, blocks),
            "turn_beyond",
            shape,
            [VMEM] * 2,
            VMEM,
            us=TURN2,
        )(pick, beyond)
        wide = pltpu.VMEM((2 * inc, 3 * blocks * 2 * block), BF16)
        windows = (second, payload, first)
        turned = (own_turned, mate_turned, beyond_turned)
        part, filled = call(
            functools.partial(near_early_kernel, sizes, inc),
            "near_early",
            (near_shape[0], jax.ShapeDtypeStruct(wide.shape, BF16)),
            [VMEM] * 6,
            (VMEM, VMEM),
            us=EARLY,
        )(*windows, *turned)
        send, last_turned = call(
            functools.partial(near_last_kernel, sizes),
            "near_last",
            (near_shape[1], shape),
            [VMEM] * 4,
            (VMEM, VMEM),
        )(pick, last, filled, part)
        keep = call(
            functools.partial(near_keep_kernel, sizes, inc),
            "near_keep",
            near_shape[0],
            [VMEM] * 7,
            VMEM,
            [wide],
        )(*windows, *turned, last_turned)
    else:
        coefs = {0: near_block.reshape(blocks, rows, slots * 2 * block)}
        bit = half // 2
        while bit:
            for at in sorted(coefs):
                coefs[at | bit] = across(coefs[at], bit)
            bit //= 2
        me = lax.axis_index("inc") % half
        stacked = jnp.stack([coefs[at] for at in range(half)], axis=1)
        stacked = jnp.take(stacked, jnp.arange(half) ^ me, axis=1)
        stacked = stacked.reshape(blocks, half * rows, slots * 2 * block)
        keep, send = call(
            functools.partial(near_rows_kernel, sizes, inc),
            "near_rows",
            near_shape,
            [SMEM] + [VMEM] * 4,
            (VMEM, VMEM),
            [wide],
        )(near_index, stacked, second, payload, first)
    bits = half if paired else 1
    got = across(send, partner)

    base, place = call(
        functools.partial(base_kernel, order, inc, bits, rows),
        "base",
        (
            jax.ShapeDtypeStruct((2 * inc, panels), F32),
            jax.ShapeDtypeStruct((block, 2 * block), BF16),
        ),
        [SMEM] * 2 + [VMEM] * (4 + panel_count),
        (VMEM, VMEM),
        [pltpu.VMEM((panel_count * blocks * rank, 2 * inc), BF16)],
    )(near_index, far_rank, field, keep, coupling, target_basis, packed, first, second, *rest)

    return call(
        final_kernel,
        "final",
        jax.ShapeDtypeStruct((2, inc, panels), BF16),
        [VMEM] * 3,
        VMEM,
    )(base, got, place)


def solution(mesh):
    return jax.shard_map(
        local,
        mesh=mesh,
        in_specs=(
            P(None, "inc", "panel"),
            P("panel", "inc", None, None, None),
            P("panel", None),
            P("panel", None, None, None),
            P("panel", None, None, None),
            P("panel", None, None, None),
            P("panel", None),
        ),
        out_specs=P(None, "inc", "panel"),
        check_vma=False,
    )
```
